256 devices in a mesh: ctx: 16 (over z_hi, x), tp: 2 (over core), ep: 8 (over y, z_lo).
Axes of the slice: x: 4, y: 4, z: 8 (z_hi: 4, z_lo: 2; z = z_hi * 2 + z_lo), core: 2. Of those that a mesh axis runs over, the one named last changes fastest.
Arguments:
- hidden: bfloat16 [2048, 3584], P('ctx'), may hold values from -40 to 40
- grad_out: bfloat16 [2048, 3584], P('ctx'), may hold values from -6 to 6
- gain: float32 [3584], replicated, may hold values from 0.5 to 1.5
- dense_gate: bfloat16 [2432, 3584], P(('tp', 'ep')), may hold values from -0.09375 to 0.09375
- dense_up: bfloat16 [2432, 3584], P(('tp', 'ep')), may hold values from -0.09375 to 0.09375
- dense_down: bfloat16 [2432, 3584], P(('tp', 'ep')), may hold values from -0.125 to 0.125
- expert_gate: bfloat16 [16, 3840, 3584], P('ctx', ('tp', 'ep')), may hold values from -0.09375 to 0.09375
- expert_up: bfloat16 [16, 3840, 3584], P('ctx', ('tp', 'ep')), may hold values from -0.09375 to 0.09375
- expert_down: bfloat16 [16, 3840, 3584], P('ctx', ('tp', 'ep')), may hold values from -0.09375 to 0.09375
- out_proj: bfloat16 [4096, 3584], P(('tp', 'ep')), may hold values from -0.09375 to 0.09375
- queries: bfloat16 [2048, 4096], P('ctx', ('tp', 'ep')), may hold values from -12 to 12
- keys: bfloat16 [2048, 4096], P('ctx', ('tp', 'ep')), may hold values from -12 to 12
- values: bfloat16 [2048, 4096], P('ctx', ('tp', 'ep')), may hold values from -6 to 6
- route_ids: int32 [2048, 2], P('ctx'), may hold values from 0 to 15, all different within a row; in each aligned block of 128 rows (0 to 127, 128 to 255, ...) at most 20 rows name the same one
- route_weights: float32 [2048, 2], P('ctx'), may hold values from 0.2 to 1
Outputs:
- grad_hidden: bfloat16 [2048, 3584], P('ctx')
- grad_queries: bfloat16 [2048, 4096], P('ctx', ('tp', 'ep'))
- grad_keys: bfloat16 [2048, 4096], P('ctx', ('tp', 'ep'))
- grad_values: bfloat16 [2048, 4096], P('ctx', ('tp', 'ep'))
The draws below stay inside these ranges and needn't reach their ends.
Inputs may be any that keep to these rules, and one draw needn't show every extreme that they name: `route_ids`: the two ids of a token differ. In each aligned block of 128 tokens no expert is named by more than 20 routed rows, a bound that some block reaches.
All inputs are finite; a program needn't handle non-finite values.
Results may differ from the reference program's by a relative error of at most 0.03.
Values may be sent and summed in bfloat16 or wider, within the bound.
No kernel may reach another device: no remote copies, remote signals or barrier semaphores. Data moves between devices by JAX's collectives and lax.ppermute only.
A program may use at most 128 MiB of HBM per device.

```python
import math
import jax
import jax.numpy as jnp
import numpy as np
from jax import lax

D = 3584
HEAD_DIM = 128
FF = 2432
EH = 3840
BLOCK = 128
SEQ = 2048
HEADS = 32
EXPERTS = 16
CAP = 20
N_CTX = 16


def draw_queries(key, part):
    key = jax.random.fold_in(key, 11)
    base = jnp.clip(jax.random.normal(key, (SEQ, HEADS * HEAD_DIM), jnp.float32), -4.0, 4.0)
    return base.astype(jnp.bfloat16)


def draw_keys(key, part):
    key = jax.random.fold_in(key, 12)
    base = jnp.clip(jax.random.normal(key, (SEQ, HEADS * HEAD_DIM), jnp.float32), -4.0, 4.0)
    return base.astype(jnp.bfloat16)


def draw_hidden(key, part):
    key = jax.random.fold_in(key, 21)
    base_key, row_key, col_key = jax.random.split(key, 3)
    row_scale = jnp.exp(jax.random.uniform(row_key, (SEQ, 1), jnp.float32, math.log(0.3), math.log(3.0)))
    col_scale = jnp.exp(jax.random.uniform(col_key, (1, D), jnp.float32, math.log(0.3), math.log(3.0)))
    base = jnp.clip(jax.random.normal(base_key, (SEQ, D), jnp.float32), -4.0, 4.0)
    return (base * row_scale * col_scale).astype(jnp.bfloat16)


def level_of(own_key, dims, cuts, low, top_value):
    loudness = 1.0
    for axis_at, parts in cuts:
        heights = jax.random.uniform(jax.random.fold_in(jax.random.fold_in(own_key, 6), axis_at), (parts,), jnp.float32, low / len(cuts), top_value / len(cuts))
        loudness = loudness * jnp.repeat(jnp.exp(heights), dims[axis_at] // parts).reshape((-1,) + (1,) * (len(dims) - 1 - axis_at))
    return loudness


def assign_block(own_key, own, number, rows, number_of, top, bound, skew):
    ranking = jax.random.permutation(own_key, number_of)
    crowded, ordinary = shares(number_of, rows * top, bound, skew, True), shares(number_of, rows * top, bound, skew, False)
    places = jnp.arange(number_of)

    def named(tallies, offset_by):
        used = int((tallies > 0).sum())
        fixed = max(1, used // 4)
        shifted = fixed + (places - fixed + offset_by * (used - fixed)) % max(1, number_of - fixed)
        return jnp.zeros((number_of,), jnp.int32).at[ranking[jnp.where(places < fixed, places, shifted)]].set(jnp.asarray(tallies, jnp.int32))

    tallies = jnp.where(number % 4 == 0, named(crowded, number // 4), named(ordinary, number - number // 4 - 1))
    mixed = jax.random.permutation(jax.random.fold_in(own, 3), number_of)
    giver, receiver = mixed[0:number_of // 2 * 2:2], mixed[1:number_of // 2 * 2:2]
    room = jnp.minimum(tallies[giver] - 1, bound - tallies[receiver]) // 2
    room = jnp.where((giver == ranking[0]) | (receiver == ranking[0]) | (tallies[receiver] == 0), 0, jnp.maximum(room, 0))
    shifted = jax.random.randint(jax.random.fold_in(own, 4), (number_of // 2,), 0, 1 << 20) % (room + 1)
    tallies = tallies.at[giver].add(-shifted).at[receiver].add(shifted)
    items = jnp.searchsorted(jnp.cumsum(tallies), jnp.arange(rows * top), side="right").astype(jnp.int32)
    table = items.reshape(top, rows).T
    table = table[jax.random.permutation(jax.random.fold_in(own, 1), rows)]
    offset_by = jax.random.randint(jax.random.fold_in(own, 2), (rows, 1), 0, top)
    return jnp.take_along_axis(table, (jnp.arange(top)[None, :] + offset_by) % top, axis=1)


def shares(amount, total, bound, skew, full):
    loads = [(1 << 20) // math.isqrt(rank ** skew) + 1 for rank in range(1, amount + 1)]
    largest = bound if full else min(bound, max(-(-total // amount), total * loads[0] // sum(loads)))
    least = 1 if total - largest >= amount - 1 else 0
    counts, surplus = [largest] + [least] * (amount - 1), total - largest - least * (amount - 1)
    while surplus > 0:
        movable = [i for i in range(1, amount) if counts[i] < largest] or [i for i in range(1, amount) if counts[i] < bound]
        pool, left = sum([loads[i] for i in movable]), surplus
        for i in movable:
            addition = min(bound - counts[i], max(1, left * loads[i] // pool), surplus)
            counts[i] = counts[i] + addition
            surplus = surplus - addition
    return np.array(counts)


def centred(key, extent, deviation, bound, pieces=(), kind=jnp.bfloat16):
    values = deviation * jax.random.normal(key, extent, jnp.float32)
    if pieces:
        values = values * level_of(key, extent, pieces, -0.22, 0.18)
    return jnp.clip(values, -bound, bound).astype(kind)


def setup_inputs(seed: int = 0) -> dict:
    seeds = jax.random.split(jax.random.key(seed), 16)
    hidden = draw_hidden(jax.random.fold_in(seeds[15], 71), 0)
    grad_out = centred(seeds[1], (SEQ, D), 1.0, 6.0, ((0, 16),))
    gain = jnp.clip(1.0 + 0.1 * jax.random.normal(seeds[2], (D,), jnp.float32), 0.5, 1.5)
    dense_gate = centred(seeds[3], (FF, D), D ** -0.5, 0.09375, ((0, 16),))
    dense_up = centred(seeds[4], (FF, D), D ** -0.5, 0.09375, ((0, 16),))
    dense_down = centred(seeds[5], (FF, D), FF ** -0.5, 0.125, ((0, 16),))
    expert_gate = centred(seeds[6], (EXPERTS, EH, D), D ** -0.5, 0.09375, ((0, 16), (1, 16)))
    expert_up = centred(seeds[7], (EXPERTS, EH, D), D ** -0.5, 0.09375, ((0, 16), (1, 16)))
    expert_down = centred(seeds[8], (EXPERTS, EH, D), EH ** -0.5, 0.09375, ((0, 16), (1, 16)))
    out_proj = centred(seeds[9], (HEADS * HEAD_DIM, D), (HEADS * HEAD_DIM) ** -0.5, 0.09375, ((0, 16),))
    queries = draw_queries(jax.random.fold_in(seeds[15], 71), 0)
    keys = draw_keys(jax.random.fold_in(seeds[15], 71), 0)
    values = centred(seeds[12], (SEQ, HEADS * HEAD_DIM), 1.0, 6.0, ((0, 16), (1, 16)))
    route_ids_keys = jax.random.split(jax.random.fold_in(seeds[13], 1), SEQ // BLOCK)
    route_ids_turns = jax.random.permutation(jax.random.fold_in(seeds[13], 3), SEQ // BLOCK)
    route_ids = jax.vmap(lambda own, number: assign_block(jax.random.fold_in(seeds[13], 2), own, number, BLOCK, EXPERTS, 2, CAP, 1))(route_ids_keys, route_ids_turns).reshape((SEQ, 2))
    route_weights = jnp.clip(0.2 + 0.8 * jax.random.uniform(seeds[14], (SEQ, 2), jnp.float32) ** level_of(seeds[14], (SEQ, 2), ((0, 16),), -0.2, 0.2), 0.2, 1.0)
    return dict(hidden=hidden, grad_out=grad_out, gain=gain, dense_gate=dense_gate, dense_up=dense_up, dense_down=dense_down, expert_gate=expert_gate, expert_up=expert_up, expert_down=expert_down, out_proj=out_proj, queries=queries, keys=keys, values=values, route_ids=route_ids, route_weights=route_weights)


NEG_FILL = -1e+30
EPSILON = 1e-05

def contract_last(left_rows, right_rows):
    return lax.dot_general(left_rows, right_rows, (((1,), (1,)), ((), ())), preferred_element_type=jnp.float32)

def swiglu_grad(inputs, upstream, w_gate, w_up, w_down):
    gate_pre = contract_last(inputs, w_gate)
    up_pre = contract_last(inputs, w_up)
    back_grad = contract_last(upstream, w_down)
    sigmoid_gate = jax.nn.sigmoid(gate_pre)
    grad_gate = (back_grad * up_pre * sigmoid_gate * (1.0 + gate_pre * (1.0 - sigmoid_gate))).astype(jnp.bfloat16)
    grad_upper = (back_grad * gate_pre * sigmoid_gate).astype(jnp.bfloat16)
    return jnp.dot(grad_gate, w_gate, preferred_element_type=jnp.float32) + jnp.dot(grad_upper, w_up, preferred_element_type=jnp.float32)

def head_grads(operands):
    query_rows, key_rows, value_rows, upstream = operands
    score_scale = HEAD_DIM ** (-0.5)
    position = lax.iota(jnp.int32, SEQ)
    allowed = position[None, :] <= position[:, None]
    scores = jnp.where(allowed, contract_last(query_rows, key_rows) * score_scale, NEG_FILL)
    top_score = lax.optimization_barrier(jnp.max(scores, axis=1, keepdims=True))
    weights = jnp.where(allowed, jnp.exp(scores - top_score), 0.0)
    weight_sum = lax.optimization_barrier(jnp.sum(weights, axis=1, keepdims=True))
    grad_probs = contract_last(upstream, value_rows)
    delta_row = lax.optimization_barrier(jnp.sum(weights * grad_probs, axis=1, keepdims=True)) / weight_sum
    log_norm = top_score + jnp.log(weight_sum)
    probs = jnp.where(allowed, jnp.exp(scores - log_norm), 0.0)
    grad_scores = probs * (grad_probs - delta_row)
    probs_half = probs.astype(jnp.bfloat16)
    grad_half = grad_scores.astype(jnp.bfloat16)
    grad_query = jnp.dot(grad_half, key_rows, preferred_element_type=jnp.float32) * score_scale
    grad_key = jnp.dot(grad_half.T, query_rows, preferred_element_type=jnp.float32) * score_scale
    grad_value = jnp.dot(probs_half.T, upstream, preferred_element_type=jnp.float32)
    return (grad_query.astype(jnp.bfloat16), grad_key.astype(jnp.bfloat16), grad_value.astype(jnp.bfloat16))

def one_expert(operands):
    return swiglu_grad(operands[0], operands[1], operands[2], operands[3], operands[4])

def per_head(array):
    return array.reshape(SEQ, HEADS, HEAD_DIM).transpose(1, 0, 2)

def merge_heads(array):
    return array.transpose(1, 0, 2).reshape(SEQ, HEADS * HEAD_DIM)

def reference(hidden, grad_out, gain, dense_gate, dense_up, dense_down, expert_gate, expert_up, expert_down, out_proj, queries, keys, values, route_ids, route_weights):
    hidden_f = hidden.astype(jnp.float32)
    inverse = lax.rsqrt(lax.optimization_barrier(jnp.mean(hidden_f * hidden_f, axis=1, keepdims=True)) + EPSILON)
    normed = hidden_f * inverse
    mixed_in = (normed * gain).astype(jnp.bfloat16)
    dense_part = swiglu_grad(mixed_in, grad_out, dense_gate, dense_up, dense_down)
    ids_block = route_ids.reshape(N_CTX, 2 * BLOCK)
    hits = (ids_block[:, :, None] == lax.iota(jnp.int32, EXPERTS)[None, None, :]).astype(jnp.int32)
    earlier = jnp.cumsum(hits, axis=1) - hits
    slots = lax.optimization_barrier(jnp.sum(earlier * hits, axis=2))
    places = ids_block * CAP + slots
    owners = lax.iota(jnp.int32, 2 * BLOCK) // 2

    def tables(place_row, weight_row):
        token_of = jnp.full((EXPERTS * CAP,), BLOCK, jnp.int32).at[place_row].set(owners)
        weight_of = jnp.zeros((EXPERTS * CAP,), jnp.float32).at[place_row].set(weight_row)
        return (token_of, weight_of)
    token_of, weight_of = jax.vmap(tables)(places, route_weights.reshape(N_CTX, 2 * BLOCK))
    present = token_of < BLOCK
    picked = jnp.minimum(token_of, BLOCK - 1) + (lax.iota(jnp.int32, N_CTX) * BLOCK)[:, None]
    send_in = jnp.where(present[:, :, None], mixed_in[picked], jnp.zeros((), jnp.bfloat16))
    send_grad = (grad_out[picked].astype(jnp.float32) * weight_of[:, :, None]).astype(jnp.bfloat16)
    expert_in = send_in.reshape(N_CTX, EXPERTS, CAP, D).transpose(1, 0, 2, 3).reshape(EXPERTS, N_CTX * CAP, D)
    expert_back = send_grad.reshape(N_CTX, EXPERTS, CAP, D).transpose(1, 0, 2, 3).reshape(EXPERTS, N_CTX * CAP, D)
    expert_rows = lax.map(one_expert, (expert_in, expert_back, expert_gate, expert_up, expert_down))
    expert_rows = expert_rows.reshape(EXPERTS, N_CTX, CAP, D).transpose(1, 0, 2, 3).reshape(N_CTX, EXPERTS * CAP, D)
    routed = jnp.take_along_axis(expert_rows, places[:, :, None], axis=1).reshape(SEQ, 2, D).sum(axis=1)
    total_grad = dense_part + routed
    scaled_grad = total_grad * gain
    grad_hidden = (grad_out.astype(jnp.float32) + inverse * (scaled_grad - normed * lax.optimization_barrier(jnp.mean(scaled_grad * normed, axis=1, keepdims=True)))).astype(jnp.bfloat16)
    grad_heads = contract_last(grad_hidden, out_proj).astype(jnp.bfloat16)
    grad_queries, grad_keys, grad_values = lax.map(head_grads, (per_head(queries), per_head(keys), per_head(values), per_head(grad_heads)))
    return (grad_hidden, merge_heads(grad_queries), merge_heads(grad_keys), merge_heads(grad_values))
```

```python
import functools

import jax
import jax.numpy as jnp
from jax import lax
from jax.experimental import pallas as pl
from jax.experimental.pallas import tpu as pltpu
from jax.sharding import PartitionSpec as P

HEAD_DIM = 128
NEG_FILL = -1e30
EPSILON = 1e-05
BF = jnp.bfloat16
F32 = jnp.float32
BLOCK = 128
D = 3584
HALF = 10
PIECE = 896
CHUNK = 256
CHUNKS = D // CHUNK
GRAY = 144
GROUPS_Z = [[4 * i + g for i in range(4)] for g in range(4)]
GROUPS_X = [[4 * g + i for i in range(4)] for g in range(4)]
VMEM = pl.BlockSpec(memory_space=pltpu.VMEM)
SMEM = pl.BlockSpec(memory_space=pltpu.SMEM)
HBM = pl.BlockSpec(memory_space=pl.ANY)


def nt(a, b):
    return lax.dot_general(a, b, (((1,), (1,)), ((), ())), preferred_element_type=F32)


def tn(a, b):
    return lax.dot_general(a, b, (((0,), (0,)), ((), ())), preferred_element_type=F32)


def nn(a, b):
    return jnp.dot(a, b, preferred_element_type=F32)


def call(kernel, out_shape, in_specs, scratch=(), mib=48, flops=0, bytes_accessed=0, name=None):
    return pl.pallas_call(
        kernel,
        out_shape=out_shape,
        in_specs=in_specs,
        out_specs=jax.tree.map(lambda _: VMEM, out_shape),
        scratch_shapes=list(scratch),
        compiler_params=pltpu.CompilerParams(vmem_limit_bytes=mib * 1024 * 1024),
        cost_estimate=pl.CostEstimate(flops=flops, bytes_accessed=bytes_accessed, transcendentals=0),
        name=name,
    )


def to_tp(x):
    return lax.ppermute(x, "tp", [(0, 1), (1, 0)])


def to_ep(x, dy, dz):
    pairs = [(y * 2 + z, ((y + dy) % 4) * 2 + (z ^ dz)) for y in range(4) for z in range(2)]
    return lax.ppermute(x, "ep", pairs)


def prepare_kernel(me, hidden, grad_out, gain, ids, weights, mixed, send, spots):
    hid = hidden[...].astype(F32)
    inverse = lax.rsqrt(jnp.mean(hid * hid, axis=1, keepdims=True) + EPSILON)
    mixed[...] = (hid * inverse * gain[...]).astype(BF)
    experts = lax.broadcasted_iota(jnp.int32, (16, BLOCK), 0)
    hit = [(ids[k : k + 1, :] == experts).astype(F32) for k in range(2)]
    before = lax.broadcasted_iota(jnp.int32, (BLOCK, BLOCK), 0) < lax.broadcasted_iota(jnp.int32, (BLOCK, BLOCK), 1)
    earlier = nn((hit[0] + hit[1]).astype(BF), before.astype(BF))
    tp = me[1]
    place_rows = lax.broadcasted_iota(jnp.int32, (512, BLOCK), 0)
    local_rows = lax.broadcasted_iota(jnp.int32, (256, BLOCK), 0) + tp * 256
    spot = jnp.zeros((512, BLOCK), F32)
    own = jnp.zeros((256, BLOCK), F32)
    own_weight = jnp.zeros((256, BLOCK), F32)
    for k in range(2):
        slot = jnp.sum(earlier * hit[k], axis=0, keepdims=True).astype(jnp.int32)
        upper = (slot >= HALF).astype(jnp.int32)
        slot = slot - HALF * upper
        name = ids[k : k + 1, :]
        spot = spot + (place_rows == name * 32 + upper * 16 + slot).astype(F32)
        mark = (local_rows == upper * 256 + name * 16 + slot).astype(F32)
        own = own + mark
        own_weight = own_weight + mark * weights[k : k + 1, :]
    spots[...] = spot.astype(BF)
    own = own.astype(BF)
    scale = jnp.sum(own_weight, axis=1, keepdims=True)
    ep = me[2]

    @pl.when(ep < 4)
    def _():
        at = pl.multiple_of(ep * PIECE, PIECE)
        send[...] = nn(own, mixed[:, pl.ds(at, PIECE)]).astype(BF)

    @pl.when(ep >= 4)
    def _():
        at = pl.multiple_of((ep - 4) * PIECE, PIECE)
        send[...] = (nn(own, grad_out[:, pl.ds(at, PIECE)]) * scale).astype(BF)


def compact_kernel(rows, out):
    to = lax.broadcasted_iota(jnp.int32, (160, 256), 0)
    at = lax.broadcasted_iota(jnp.int32, (160, 256), 1)
    block = at // 16
    slot = at - block * 16
    pick = ((to == block * HALF + slot) & (slot < HALF)).astype(BF)
    out[...] = nn(pick, rows[...]).astype(BF)


def hidden_grads(x, y, gate, up, down):
    a = nt(x, gate)
    b = nt(x, up)
    back = nt(y, down)
    s = jax.nn.sigmoid(a)
    ga = (back * b * s * (1.0 + a * (1.0 - s))).astype(BF)
    gb = (back * a * s).astype(BF)
    return ga, gb


def chunk_lanes(chunk):
    return pl.ds(pl.multiple_of(jnp.minimum(chunk, CHUNKS - 1) * CHUNK, CHUNK), CHUNK)


def dense_kernel(mixed, grad_out, gate, up, down, out):
    ga, gb = hidden_grads(mixed[...], grad_out[...], gate[...], up[...], down[...])
    for c in range(CHUNKS):
        lanes = slice(c * CHUNK, (c + 1) * CHUNK)
        out[c] = (nn(ga, gate[:, lanes]) + nn(gb, up[:, lanes])).astype(BF)
    for c in range(CHUNKS, 16):
        out[c] = jnp.zeros((BLOCK, CHUNK), BF)


def expert_kernel(me, *refs):
    blocks, (gate, up, down, mine, other, rows, sems) = refs[:16], refs[16:]
    tp, ep = me[1], me[2]
    y, z = ep // 2, ep % 2
    z_other = 1 - z
    sources = [(0, z), (0, z_other), (3, z), (1, z_other), (1, z), (3, z_other), (2, z), (2, z_other)]
    copies = []
    for n, block in enumerate(blocks):
        dy, source_z = sources[n % 8]
        source = ((y + dy) % 4) * 2 + source_z
        core = tp if n < 8 else 1 - tp
        target = rows.at[
            pl.ds(pl.multiple_of(core * 160, 160), 160), pl.ds(pl.multiple_of(source * PIECE, PIECE), PIECE)
        ]
        copies.append(pltpu.make_async_copy(block, target, sems.at[n]))
    for copy in copies:
        copy.start()
    for copy in copies:
        copy.wait()
    ga, gb = hidden_grads(rows[:, :D], rows[:, D:], gate[...], up[...], down[...])
    for half, out in ((1 - tp, other), (tp, mine)):
        for d in range(4):
            for zz in range(2):
                lanes = chunk_lanes(half * 8 + ((y + d) % 4) * 2 + zz)
                out[d, zz] = (nn(ga, gate[:, lanes]) + nn(gb, up[:, lanes])).astype(BF)


def sum_kernel(me, first, second, third, fourth, keep, give):
    z = me[2] % 2
    for at, out in ((z, keep), (1 - z, give)):
        total = (
            first[at].astype(F32) + second[at].astype(F32) + third[at].astype(F32) + fourth[at].astype(F32)
        )
        out[...] = total.astype(BF)


def expand_kernel(keep, came, out):
    total = (keep[...].astype(F32) + came[...].astype(F32)).astype(BF)
    to = lax.broadcasted_iota(jnp.int32, (512, 320), 0)
    at = lax.broadcasted_iota(jnp.int32, (512, 320), 1)
    block = to // 32
    core = (to - block * 32) // 16
    slot = to - block * 32 - core * 16
    pick = ((at == core * 160 + block * HALF + slot) & (slot < HALF)).astype(BF)
    out[...] = nn(pick, total).astype(BF)


def combine_kernel(spots, rows, dense, out):
    total = (tn(spots[...], rows[...]) + dense[...].astype(F32)).astype(BF)
    for n in range(8):
        out[n] = total


def split3(x):
    hi = x.astype(BF).astype(F32)
    mid = (x - hi).astype(BF).astype(F32)
    return hi, mid, x - hi - mid


def norm_kernel(me, hidden, grad_out, gain, mine, other, out_proj, stats, heads_out, grad_hidden, message, total):
    tp = me[1]
    for n in range(8):
        total[:, pl.ds(pl.multiple_of((tp * 8 + n) * CHUNK, CHUNK), CHUNK)] = mine[n]
        total[:, pl.ds(pl.multiple_of(((1 - tp) * 8 + n) * CHUNK, CHUNK), CHUNK)] = other[n]
    hid = hidden[...].astype(F32)
    inverse = lax.rsqrt(jnp.mean(hid * hid, axis=1, keepdims=True) + EPSILON)
    normed = hid * inverse
    scaled = total[:, :D].astype(F32) * gain[...]
    mean = jnp.mean(scaled * normed, axis=1, keepdims=True)
    grad = (grad_out[...].astype(F32) + inverse * (scaled - normed * mean)).astype(BF)
    grad_hidden[...] = grad
    heads = nt(grad, out_proj[...]).astype(BF)
    heads_t = nt(out_proj[...], grad).astype(BF).astype(F32)
    rows = []
    for h in range(2):
        delta = jnp.sum(heads_t[h * HEAD_DIM : (h + 1) * HEAD_DIM] * heads_out[h], axis=0, keepdims=True)
        rows.append(list(split3(stats[h : h + 1, :])) + list(split3(delta)))
    for n in range(4):
        message[n, :BLOCK, :] = heads
    extra = jnp.concatenate(
        [jnp.concatenate([rows[0][k], rows[1][k]], axis=1) for k in range(6)] + [jnp.zeros((10, 256), F32)], axis=0
    ).astype(BF)
    for n in range(4):
        message[n, BLOCK:, :] = extra


def stats_kernel(me, own, gathered, stats, heads_out):
    block = me[0]
    key_at = lax.broadcasted_iota(jnp.int32, (2048, BLOCK), 0)
    query_at = lax.broadcasted_iota(jnp.int32, (2048, BLOCK), 1) + block * BLOCK
    allowed = key_at <= query_at
    lines = []
    for h in range(2):
        lanes = slice(h * HEAD_DIM, (h + 1) * HEAD_DIM)
        keys = gathered[:, 256 + h * HEAD_DIM : 256 + (h + 1) * HEAD_DIM]
        values = gathered[:, 512 + h * HEAD_DIM : 512 + (h + 1) * HEAD_DIM]
        scores = jnp.where(allowed, nt(keys, own[:, lanes]) * HEAD_DIM ** (-0.5), NEG_FILL)
        top = jnp.max(scores, axis=0, keepdims=True)
        weights = jnp.where(allowed, jnp.exp(scores - top), 0.0)
        lines.append(top + jnp.log(jnp.sum(weights, axis=0, keepdims=True)))
        half = weights.astype(BF)
        heads_out[h] = tn(values, half) / jnp.sum(half.astype(F32), axis=0, keepdims=True)
    stats[...] = jnp.concatenate(lines + [jnp.zeros((6, BLOCK), F32)], axis=0)


def attention_kernel(me, own_q, gathered, grads, grad_q, grad_k, grad_v, sum_q, sum_k, sum_v):
    block = me[0]
    scale = HEAD_DIM ** (-0.5)
    sum_q[...] = jnp.zeros_like(sum_q)
    sum_k[...] = jnp.zeros_like(sum_k)
    sum_v[...] = jnp.zeros_like(sum_v)
    own_rows = pl.ds(pl.multiple_of(block * BLOCK, BLOCK), BLOCK)
    x, z = block % 4, block // 4
    below = lax.broadcasted_iota(jnp.int32, (BLOCK, BLOCK), 0) <= lax.broadcasted_iota(jnp.int32, (BLOCK, BLOCK), 1)

    def pair(h, keys, values, queries, upstream, extra, allowed):
        at = slice(h * HEAD_DIM, (h + 1) * HEAD_DIM)
        line = extra[:, at].astype(F32)
        log_norm = line[0:1] + line[1:2] + line[2:3]
        delta = line[3:4] + line[4:5] + line[5:6]
        probs = jnp.exp(nt(keys, queries) * scale - log_norm)
        if allowed is not None:
            probs = jnp.where(allowed, probs, 0.0)
        grad_scores = probs * (nt(values, upstream) - delta)
        return probs.astype(BF), grad_scores.astype(BF)

    def keys_of(rows, h):
        return gathered[rows, 256 + h * HEAD_DIM : 256 + (h + 1) * HEAD_DIM]

    def values_of(rows, h):
        return gathered[rows, 512 + h * HEAD_DIM : 512 + (h + 1) * HEAD_DIM]

    own_extra = grads[x, z, BLOCK:, :]
    for i in range(16):
        rows = slice(i * BLOCK, (i + 1) * BLOCK)

        @pl.when(i < block)
        def _(rows=rows):
            for h in range(2):
                at = slice(h * HEAD_DIM, (h + 1) * HEAD_DIM)
                keys = keys_of(rows, h)
                _, half = pair(h, keys, values_of(rows, h), own_q[:, at], grads[x, z, :BLOCK, at], own_extra, None)
                sum_q[:, at] += tn(half, keys)

        @pl.when(i > block)
        def _(i=i, rows=rows):
            extra = grads[i % 4, i // 4, BLOCK:, :]
            for h in range(2):
                at = slice(h * HEAD_DIM, (h + 1) * HEAD_DIM)
                queries = gathered[rows, at]
                upstream = grads[i % 4, i // 4, :BLOCK, at]
                probs, half = pair(h, keys_of(own_rows, h), values_of(own_rows, h), queries, upstream, extra, None)
                sum_k[:, at] += nn(half, queries)
                sum_v[:, at] += nn(probs, upstream)

    for h in range(2):
        at = slice(h * HEAD_DIM, (h + 1) * HEAD_DIM)
        keys = keys_of(own_rows, h)
        queries = own_q[:, at]
        upstream = grads[x, z, :BLOCK, at]
        probs, half = pair(h, keys, values_of(own_rows, h), queries, upstream, own_extra, below)
        grad_q[:, at] = ((sum_q[:, at] + tn(half, keys)) * scale).astype(BF)
        grad_k[:, at] = ((sum_k[:, at] + nn(half, queries)) * scale).astype(BF)
        grad_v[:, at] = (sum_v[:, at] + nn(probs, upstream)).astype(BF)


def shape(*dims, kind=BF):
    return jax.ShapeDtypeStruct(dims, kind)


def body(
    hidden,
    grad_out,
    gain,
    dense_gate,
    dense_up,
    dense_down,
    expert_gate,
    expert_up,
    expert_down,
    out_proj,
    queries,
    keys,
    values,
    route_ids,
    route_weights,
):
    me = jnp.stack([lax.axis_index("ctx"), lax.axis_index("tp"), lax.axis_index("ep")]).astype(jnp.int32)
    gain_row = gain.reshape(1, D)
    gathered = lax.all_gather(jnp.concatenate([queries, keys, values], axis=1), "ctx", axis=0, tiled=True)

    mixed, send, spots = call(
        prepare_kernel,
        (shape(BLOCK, D), shape(256, PIECE), shape(512, BLOCK)),
        [SMEM] + [VMEM] * 5,
        flops=10**8,
        bytes_accessed=4 * 10**6,
        name="prepare",
    )(me, hidden, grad_out, gain_row, route_ids.T, route_weights.T)
    came = lax.all_to_all(send.reshape(16, 16, PIECE), "ctx", split_axis=0, concat_axis=0, tiled=True)

    dense = call(
        dense_kernel,
        shape(16, BLOCK, CHUNK),
        [VMEM] * 5,
        flops=10 * 128 * 152 * D,
        bytes_accessed=6 * 10**6,
        name="dense",
    )(mixed, grad_out, dense_gate, dense_up, dense_down)
    dense = lax.psum_scatter(dense, ("tp", "ep"), scatter_dimension=0, tiled=True)[0]

    piece = call(compact_kernel, shape(160, PIECE), [VMEM], name="compact")(came.reshape(256, PIECE))
    across = to_ep(piece, 0, 1)
    right, across_left = to_ep(piece, 1, 0), to_ep(across, -1, 0)
    left, across_right = to_ep(piece, -1, 0), to_ep(across, 1, 0)
    far, across_far = to_ep(right, 1, 0), to_ep(across_left, -1, 0)
    pieces = [piece, across, right, across_left, left, across_right, far, across_far]
    pieces = pieces + [to_tp(p) for p in pieces]
    mine, other = call(
        expert_kernel,
        (shape(4, 2, 320, CHUNK), shape(4, 2, 320, CHUNK)),
        [SMEM] + [HBM] * 16 + [VMEM] * 3,
        scratch=[pltpu.VMEM((320, 2 * D), BF), pltpu.SemaphoreType.DMA((16,))],
        flops=10 * 320 * 240 * D,
        bytes_accessed=13 * 10**6,
        name="expert",
    )(me, *pieces, expert_gate[0], expert_up[0], expert_down[0])
    other = to_tp(other)
    first, second, third, fourth = [
        (mine[d].astype(F32) + other[d].astype(F32)).astype(BF) for d in range(4)
    ]
    keep, give = call(
        sum_kernel,
        (shape(320, CHUNK), shape(320, CHUNK)),
        [SMEM] + [VMEM] * 4,
        name="sum",
    )(me, first, to_ep(second, 1, 0), to_ep(fourth, -1, 0), to_ep(third, 2, 0))
    back = call(expand_kernel, shape(512, CHUNK), [VMEM] * 2, name="expand")(keep, to_ep(give, 0, 1))
    back = lax.all_to_all(back.reshape(16, 32, CHUNK), "ctx", split_axis=0, concat_axis=0, tiled=True)

    stats, heads_out = call(
        stats_kernel,
        (shape(8, BLOCK, kind=F32), shape(2, HEAD_DIM, BLOCK, kind=F32)),
        [SMEM] + [VMEM] * 2,
        flops=4 * 2 * 2048 * 128 * 128,
        bytes_accessed=4 * 10**6,
        name="stats",
    )(me, queries, gathered)

    total = call(combine_kernel, shape(8, BLOCK, CHUNK), [VMEM] * 3, name="combine")(
        spots, back.reshape(512, CHUNK), dense
    )
    total = lax.all_to_all(total, "ep", split_axis=0, concat_axis=0, tiled=True)
    grad_hidden, message = call(
        norm_kernel,
        (shape(BLOCK, D), shape(4, GRAY, 256)),
        [SMEM] + [VMEM] * 8,
        scratch=[pltpu.VMEM((BLOCK, 16 * CHUNK), BF)],
        flops=4 * 128 * 256 * D,
        bytes_accessed=6 * 10**6,
        name="norm",
    )(me, hidden, grad_out, gain_row, total, to_tp(total), out_proj, stats, heads_out)
    message = lax.all_to_all(
        message, "ctx", split_axis=0, concat_axis=0, tiled=True, axis_index_groups=GROUPS_Z
    )
    message = lax.optimization_barrier(jnp.broadcast_to(message[None], (4, 4, GRAY, 256)))
    message = lax.all_to_all(
        message, "ctx", split_axis=0, concat_axis=0, tiled=True, axis_index_groups=GROUPS_X
    )
    grad_q, grad_k, grad_v = call(
        attention_kernel,
        (shape(BLOCK, 256),) * 3,
        [SMEM] + [VMEM] * 3,
        scratch=[pltpu.VMEM((BLOCK, 256), F32)] * 3,
        flops=17 * 2 * 5 * 2 * 128**3,
        bytes_accessed=5 * 10**6,
        name="attention",
    )(me, queries, gathered, message)
    return grad_hidden, grad_q, grad_k, grad_v


def solution(mesh):
    return jax.shard_map(
        body,
        mesh=mesh,
        in_specs=(
            P("ctx", None),
            P("ctx", None),
            P(),
            P(("tp", "ep"), None),
            P(("tp", "ep"), None),
            P(("tp", "ep"), None),
            P("ctx", ("tp", "ep"), None),
            P("ctx", ("tp", "ep"), None),
            P("ctx", ("tp", "ep"), None),
            P(("tp", "ep"), None),
            P("ctx", ("tp", "ep")),
            P("ctx", ("tp", "ep")),
            P("ctx", ("tp", "ep")),
            P("ctx", None),
            P("ctx", None),
        ),
        out_specs=(
            P("ctx", None),
            P("ctx", ("tp", "ep")),
            P("ctx", ("tp", "ep")),
            P("ctx", ("tp", "ep")),
        ),
        check_vma=False,
    )
```

```python
import functools

import jax
import jax.numpy as jnp
from jax import lax
from jax.experimental import pallas as pl
from jax.experimental.pallas import tpu as pltpu
from jax.sharding import PartitionSpec as P

HEAD_DIM = 128
NEG_FILL = -1e30
EPSILON = 1e-05
BF = jnp.bfloat16
F32 = jnp.float32
BLOCK = 128
D = 3584
HALF = 10
PIECE = 896
CHUNK = 512
STRIDE = 24
SCALE = HEAD_DIM ** (-0.5)
CHUNKS = D // CHUNK
GRAY = 144
VMEM = pl.BlockSpec(memory_space=pltpu.VMEM)
SMEM = pl.BlockSpec(memory_space=pltpu.SMEM)
HBM = pl.BlockSpec(memory_space=pltpu.HBM)


def nt(a, b):
    return lax.dot_general(a, b, (((1,), (1,)), ((), ())), preferred_element_type=F32)


def tn(a, b):
    return lax.dot_general(a, b, (((0,), (0,)), ((), ())), preferred_element_type=F32)


def nn(a, b):
    return jnp.dot(a, b, preferred_element_type=F32)


def call(kernel, out_shape, in_specs, scratch=(), mib=12, flops=0, bytes_accessed=0, name=None):
    return pl.pallas_call(
        kernel,
        out_shape=out_shape,
        in_specs=in_specs,
        out_specs=jax.tree.map(lambda _: VMEM, out_shape),
        scratch_shapes=list(scratch),
        compiler_params=pltpu.CompilerParams(vmem_limit_bytes=mib * 1024 * 1024),
        cost_estimate=pl.CostEstimate(flops=flops, bytes_accessed=bytes_accessed, transcendentals=0),
        name=name,
    )


def in_hbm(x):
    return pltpu.with_memory_space_constraint(x, pltpu.HBM)


def in_vmem(x):
    return pltpu.with_memory_space_constraint(x, pltpu.VMEM)


def to_tp(x):
    return lax.ppermute(x, "tp", [(0, 1), (1, 0)])


def to_ep(x, dy, dz):
    pairs = [(y * 2 + z, ((y + dy) % 4) * 2 + (z ^ dz)) for y in range(4) for z in range(2)]
    return lax.ppermute(x, "ep", pairs)


def to_ctx(x, dz, dx):
    pairs = [
        (z * 4 + q, (z + dz) * 4 + (q + dx) % 4) for z in range(4) for q in range(4) if 0 <= z + dz < 4
    ]
    return lax.ppermute(x, "ctx", pairs)


def sum_over_y(me, parts, name):
    size = shape(parts[0].shape[0], CHUNK)
    return call(sum_kernel, (size, size), [SMEM] + [VMEM] * 4, name=name)(
        me, parts[0], to_ep(parts[1], 1, 0), to_ep(parts[3], -1, 0), to_ep(parts[2], 2, 0)
    )


def prepare_kernel(
    me, hidden, grad_out, gain, ids, weights, queries, keys, values, mixed, send, spots, heads, hid_rows, grad_rows, sems
):
    copies = []
    for n in range(8):
        part = pl.ds(n * 16, 16)
        copies.append(pltpu.make_async_copy(hidden.at[part], hid_rows.at[part], sems.at[n]))
        copies[-1].start()
    lanes = pl.ds(pl.multiple_of((me[2] // 2 % 2) * 2 * PIECE, 2 * PIECE), 2 * PIECE)
    for n in range(4):
        part = pl.ds(n * 32, 32)
        copies.append(pltpu.make_async_copy(grad_out.at[part, lanes], grad_rows.at[part], sems.at[8 + n]))
        copies[-1].start()
    for n, source in enumerate((queries, keys, values)):
        copies.append(pltpu.make_async_copy(source, heads.at[:, pl.ds(n * 256, 256)], sems.at[12 + n]))
        copies[-1].start()
    tp = me[1]
    y = me[2] // 2
    experts = lax.broadcasted_iota(jnp.int32, (16, BLOCK), 0)
    hit = [(ids[k : k + 1, :] == experts).astype(F32) for k in range(2)]
    before = lax.broadcasted_iota(jnp.int32, (BLOCK, BLOCK), 0) < lax.broadcasted_iota(jnp.int32, (BLOCK, BLOCK), 1)
    earlier = nn((hit[0] + hit[1]).astype(BF), before.astype(BF))
    place_rows = lax.broadcasted_iota(jnp.int32, (256, BLOCK), 0)
    send_rows = lax.broadcasted_iota(jnp.int32, (16 * STRIDE, BLOCK), 0)
    spot = jnp.zeros((256, BLOCK), F32)
    own = [jnp.zeros((16 * STRIDE, BLOCK), F32) for _ in range(2)]
    weight = jnp.zeros((16 * STRIDE, BLOCK), F32)
    for k in range(2):
        slot = jnp.sum(earlier * hit[k], axis=0, keepdims=True).astype(jnp.int32)
        upper = (slot >= HALF).astype(jnp.int32)
        slot = slot - HALF * upper
        name = ids[k : k + 1, :]
        away = jnp.where(upper == tp, 0, 4096)
        spot = spot + (place_rows == name * 16 + slot + away).astype(F32)
        for h in range(2):
            mark = (send_rows == name * STRIDE + h * HALF + slot + away).astype(F32)
            own[h] = own[h] + mark
            weight = weight + mark * weights[k : k + 1, :]
    spots[...] = spot.astype(BF)
    scale = jnp.sum(weight, axis=1, keepdims=True)
    own = [o.astype(BF) for o in own]
    for n in range(8):
        copies[n].wait()
        part = slice(n * 16, (n + 1) * 16)
        hid = hid_rows[part, :].astype(F32)
        inverse = lax.rsqrt(jnp.mean(hid * hid, axis=1, keepdims=True) + EPSILON)
        mixed[part, :] = (hid * inverse * gain[...][None, :]).astype(BF)
    for copy in copies[8:]:
        copy.wait()

    @pl.when(y < 2)
    def _():
        at = (y % 2) * 2 * PIECE
        first = pl.ds(pl.multiple_of(at, PIECE), PIECE)
        second = pl.ds(pl.multiple_of(at + PIECE, PIECE), PIECE)
        rows = nn(own[0], mixed[:, first]) + nn(own[1], mixed[:, second])
        send[...] = rows.reshape(16, STRIDE, PIECE).astype(BF)

    @pl.when(y >= 2)
    def _():
        rows = (nn(own[0], grad_rows[:, :PIECE]) + nn(own[1], grad_rows[:, PIECE:])) * scale
        send[...] = rows.reshape(16, STRIDE, PIECE).astype(BF)


def compact_kernel(came, out):
    rows = came[...].astype(F32).reshape(16 * STRIDE, PIECE).astype(BF)
    to = lax.broadcasted_iota(jnp.int32, (320, 16 * STRIDE), 0)
    at = lax.broadcasted_iota(jnp.int32, (320, 16 * STRIDE), 1)
    block = at // STRIDE
    place = at - block * STRIDE
    half = (place >= HALF).astype(jnp.int32)
    pick = ((to == half * 160 + block * HALF + place - half * HALF) & (place < 2 * HALF)).astype(BF)
    out[...] = nn(pick, rows).astype(BF)


def hidden_grads(x, y, gate, up, down):
    a = nt(x, gate)
    b = nt(x, up)
    back = nt(y, down)
    s = jax.nn.sigmoid(a)
    ga = (back * b * s * (1.0 + a * (1.0 - s))).astype(BF)
    gb = (back * a * s).astype(BF)
    return ga, gb


def piece_lanes(index):
    return pl.ds(pl.multiple_of(index * PIECE, PIECE), PIECE)


def dense_kernel(me, mixed, grad_out, gate_in, up_in, down_in, *refs):
    outs, (grad_rows, gate, up, down, sems) = refs[:4], refs[4:]
    copies = []
    for source, target in ((gate_in, gate), (up_in, up), (down_in, down), (grad_out, grad_rows)):
        for start in range(0, D, PIECE):
            part = pl.ds(start, PIECE)
            copies.append(pltpu.make_async_copy(source.at[:, part], target.at[:, part], sems.at[len(copies)]))
    for copy in copies:
        copy.start()
    for copy in copies:
        copy.wait()
    y = me[2] // 2
    ga, gb = hidden_grads(mixed[...], grad_rows[...], gate[...], up[...], down[...])
    for d, out in enumerate(outs):
        lanes = piece_lanes((y + d) % 4)
        out[...] = (nn(ga, gate[:, lanes]) + nn(gb, up[:, lanes])).astype(BF)


def expert_kernel(me, own, right, left, far0, far1, gate, up, down, gate2, up2, down2, *refs):
    outs, (rows, sems) = refs[:4], refs[4:]
    y = me[2] // 2

    def copy(block, from_row, dy, h, n):
        target = rows.at[:, piece_lanes(((y + dy) % 4) * 2 + h)]
        return pltpu.make_async_copy(block.at[pl.ds(from_row, 160)], target, sems.at[n])

    copies = [
        copy(own, 0, 0, 0, 0),
        copy(own, 160, 0, 1, 1),
        copy(right, 0, 3, 0, 2),
        copy(right, 160, 3, 1, 3),
        copy(left, 0, 1, 0, 4),
        copy(left, 160, 1, 1, 5),
        copy(far0, 0, 2, 0, 6),
        copy(far1, 0, 2, 1, 7),
    ]
    for c in copies:
        c.start()
    for c in copies:
        c.wait()
    x, g = rows[:, :D], rows[:, D:]
    ga, gb = hidden_grads(x, g, gate[...], up[...], down[...])
    ga2, gb2 = hidden_grads(x, g, gate2[...], up2[...], down2[...])
    for d, out in enumerate(outs):
        lanes = piece_lanes((y + d) % 4)
        total = nn(ga, gate[:, lanes]) + nn(gb, up[:, lanes])
        total = total + (nn(ga2, gate2[:, lanes]) + nn(gb2, up2[:, lanes]))
        out[...] = total.astype(BF)


def sum_kernel(me, first, second, third, fourth, keep, give):
    z = me[2] % 2
    for side, out in ((z, keep), (1 - z, give)):
        lanes = pl.ds(pl.multiple_of(side * (PIECE - CHUNK), 128), CHUNK)
        total = first[:, lanes].astype(F32) + second[:, lanes].astype(F32)
        total = total + third[:, lanes].astype(F32) + fourth[:, lanes].astype(F32)
        out[...] = total.astype(BF)


def expand_kernel(keep, came, out):
    total = (keep[...].astype(F32) + came[...].astype(F32)).astype(BF)
    to = lax.broadcasted_iota(jnp.int32, (256, 160), 0)
    at = lax.broadcasted_iota(jnp.int32, (256, 160), 1)
    block = to // 16
    slot = to - block * 16
    pick = ((at == block * HALF + slot) & (slot < HALF)).astype(BF)
    out[...] = nn(pick, total).astype(BF)


def combine_kernel(me, spots, rows, dense_keep, dense_came, keep, give):
    tp = me[1]
    for half, out in ((tp, keep), (1 - tp, give)):
        lanes = pl.ds(pl.multiple_of(half * 256, 256), 256)
        total = tn(spots[...], rows[:, lanes]) + dense_keep[:, lanes].astype(F32) + dense_came[:, lanes].astype(F32)
        out[...] = total.astype(out.dtype)


def split3(x):
    hi = x.astype(BF).astype(F32)
    mid = (x - hi).astype(BF).astype(F32)
    return hi, mid, x - hi - mid


def norm_kernel(
    me, hidden, grad_out, gain, mine, other, proj_in, stats, heads_out, grad_hidden, message, total, out_proj, sems
):
    copies = []
    for n in range(8):
        part = pl.ds(n * 32, 32)
        copies.append(pltpu.make_async_copy(proj_in.at[part], out_proj.at[part], sems.at[n]))
        copies[-1].start()
    tp = me[1]
    for n in range(8):
        at = (n // 2) * PIECE + (n % 2) * (PIECE - CHUNK)
        total[:, pl.ds(pl.multiple_of(at + tp * 256, 128), 256)] = mine[n]
        total[:, pl.ds(pl.multiple_of(at + (1 - tp) * 256, 128), 256)] = other[n]
    hid = hidden[...].astype(F32)
    inverse = lax.rsqrt(jnp.mean(hid * hid, axis=1, keepdims=True) + EPSILON)
    normed = hid * inverse
    scaled = total[...].astype(F32) * gain[...][None, :]
    mean = jnp.mean(scaled * normed, axis=1, keepdims=True)
    grad = (grad_out[...].astype(F32) + inverse * (scaled - normed * mean)).astype(BF)
    grad_hidden[...] = grad
    for copy in copies:
        copy.wait()
    heads = nt(grad, out_proj[...]).astype(BF)
    heads_t = nt(out_proj[...], grad).astype(BF).astype(F32)
    rows = []
    for h in range(2):
        delta = jnp.sum(heads_t[h * HEAD_DIM : (h + 1) * HEAD_DIM] * heads_out[h], axis=0, keepdims=True)
        rows.append(list(split3(stats[h : h + 1, :])) + list(split3(delta)))
    message[:BLOCK, :] = heads
    message[BLOCK:, :] = jnp.concatenate(
        [jnp.concatenate([rows[0][k], rows[1][k]], axis=1) for k in range(6)] + [jnp.zeros((10, 256), F32)], axis=0
    ).astype(BF)


def stats_kernel(me, own, gathered, stats, heads_out):
    block = me[0]
    key_at = lax.broadcasted_iota(jnp.int32, (2048, BLOCK), 0)
    query_at = lax.broadcasted_iota(jnp.int32, (2048, BLOCK), 1) + block * BLOCK
    allowed = key_at <= query_at
    lines = []
    for h in range(2):
        lanes = slice(h * HEAD_DIM, (h + 1) * HEAD_DIM)
        keys = gathered[:, 256 + h * HEAD_DIM : 256 + (h + 1) * HEAD_DIM]
        values = gathered[:, 512 + h * HEAD_DIM : 512 + (h + 1) * HEAD_DIM]
        scores = jnp.where(allowed, nt(keys, own[:, lanes]) * HEAD_DIM ** (-0.5), NEG_FILL)
        top = jnp.max(scores, axis=0, keepdims=True)
        weights = jnp.where(allowed, jnp.exp(scores - top), 0.0)
        lines.append(top + jnp.log(jnp.sum(weights, axis=0, keepdims=True)))
        half = weights.astype(BF)
        heads_out[h] = tn(values, half) / jnp.sum(half.astype(F32), axis=0, keepdims=True)
    stats[...] = jnp.concatenate(lines + [jnp.zeros((6, BLOCK), F32)], axis=0)


def pair(keys, values, queries, upstream, lines, allowed):
    log_norm = lines[0:1] + lines[1:2] + lines[2:3]
    delta = lines[3:4] + lines[4:5] + lines[5:6]
    probs = jnp.where(allowed, jnp.exp(nt(keys, queries) * SCALE - log_norm), 0.0)
    grad_scores = probs * (nt(values, upstream) - delta)
    return probs.astype(BF), grad_scores.astype(BF)


def head(h, start=0):
    return slice(start + h * HEAD_DIM, start + (h + 1) * HEAD_DIM)


def queries_kernel(me, own_q, gathered, message, grad_q, total):
    block = me[0]
    lines = message[BLOCK:, :].astype(F32)
    query_at = lax.broadcasted_iota(jnp.int32, (512, BLOCK), 1) + block * BLOCK
    total[...] = jnp.zeros_like(total)
    for i in range(4):

        @pl.when(4 * i <= block)
        def _(i=i):
            rows = slice(i * 512, (i + 1) * 512)
            allowed = lax.broadcasted_iota(jnp.int32, (512, BLOCK), 0) + i * 512 <= query_at
            for h in range(2):
                keys = gathered[rows, head(h, 256)]
                values = gathered[rows, head(h, 512)]
                _, half = pair(keys, values, own_q[:, head(h)], message[:BLOCK, head(h)], lines[:, head(h)], allowed)
                total[:, head(h)] += tn(half, keys)

    grad_q[...] = (total[...] * SCALE).astype(BF)


def keys_kernel(shifts, first, last, me, gathered, *refs):
    count = len(shifts)
    grads, refs = refs[:count], refs[count:]
    if first:
        out_k, out_v, sum_k, sum_v = refs
        sum_k[...] = jnp.zeros_like(sum_k)
        sum_v[...] = jnp.zeros_like(sum_v)
    else:
        in_k, in_v, out_k, out_v, sum_k, sum_v = refs
        sum_k[...] = in_k[...]
        sum_v[...] = in_v[...]
    block = me[0]
    x, z = block % 4, block // 4
    own_rows = pl.ds(pl.multiple_of(block * BLOCK, BLOCK), BLOCK)
    lane = lax.broadcasted_iota(jnp.int32, (BLOCK, 4 * BLOCK), 1)
    key_at = lax.broadcasted_iota(jnp.int32, (BLOCK, 4 * BLOCK), 0) + block * BLOCK
    row = z + lane // BLOCK
    for shift, source in zip(shifts, grads):
        column = (x + shift) % 4
        allowed = (row < 4) & (key_at <= (row * 4 + column) * BLOCK + lane % BLOCK)
        blocks = [jnp.minimum((z + n) * 4 + column, 15) for n in range(4)]
        queries = jnp.concatenate(
            [gathered[pl.ds(pl.multiple_of(i * BLOCK, BLOCK), BLOCK), :256] for i in blocks], axis=0
        )
        upstream = jnp.concatenate([source[n, :BLOCK, :] for n in range(4)], axis=0)
        lines = [source[n, BLOCK:, :].astype(F32) for n in range(4)]
        for h in range(2):
            line = jnp.concatenate([part[:, head(h)] for part in lines], axis=1)
            keys = gathered[own_rows, head(h, 256)]
            values = gathered[own_rows, head(h, 512)]
            probs, half = pair(keys, values, queries[:, head(h)], upstream[:, head(h)], line, allowed)
            sum_k[:, head(h)] += nn(half, queries[:, head(h)])
            sum_v[:, head(h)] += nn(probs, upstream[:, head(h)])

    if last:
        out_k[...] = (sum_k[...] * SCALE).astype(BF)
        out_v[...] = sum_v[...].astype(BF)
    else:
        out_k[...] = sum_k[...]
        out_v[...] = sum_v[...]


def shape(*dims, kind=BF):
    return jax.ShapeDtypeStruct(dims, kind)


def body(
    hidden,
    grad_out,
    gain,
    dense_gate,
    dense_up,
    dense_down,
    expert_gate,
    expert_up,
    expert_down,
    out_proj,
    queries,
    keys,
    values,
    route_ids,
    route_weights,
):
    me = jnp.stack([lax.axis_index("ctx"), lax.axis_index("tp"), lax.axis_index("ep")]).astype(jnp.int32)
    experts = [expert_gate[0], expert_up[0], expert_down[0]]

    mixed, send, spots, heads = call(
        prepare_kernel,
        (shape(BLOCK, D), shape(16, STRIDE, PIECE), shape(256, BLOCK), shape(BLOCK, 768)),
        [SMEM, HBM, HBM, VMEM, VMEM, VMEM, HBM, HBM, HBM],
        scratch=[pltpu.VMEM((BLOCK, D), BF), pltpu.VMEM((BLOCK, 2 * PIECE), BF), pltpu.SemaphoreType.DMA((15,))],
        flops=10**8,
        bytes_accessed=4 * 10**6,
        mib=16,
        name="prepare",
    )(me, in_hbm(hidden), in_hbm(grad_out), gain, route_ids.T, route_weights.T, *[in_hbm(w) for w in (queries, keys, values)])
    gathered = lax.all_gather(heads, "ctx", axis=0, tiled=True)
    came = lax.all_to_all(send, "ctx", split_axis=0, concat_axis=0, tiled=True)

    dense = call(
        dense_kernel,
        (shape(BLOCK, PIECE),) * 4,
        [SMEM, VMEM] + [HBM] * 4,
        scratch=[pltpu.VMEM((BLOCK, D), BF)] + [pltpu.VMEM((152, D), BF)] * 3 + [pltpu.SemaphoreType.DMA((16,))],
        flops=10 * 128 * 152 * D,
        bytes_accessed=6 * 10**6,
        mib=16,
        name="dense",
    )(me, mixed, *[in_hbm(w) for w in (grad_out, dense_gate, dense_up, dense_down)])
    peers = [to_tp(w) for w in experts]
    dense_keep, dense_give = sum_over_y(me, dense, "dense_sum")

    came, dense_keep, dense_give, peers = lax.optimization_barrier((came, dense_keep, dense_give, peers))
    own = call(compact_kernel, shape(320, PIECE), [VMEM], name="compact")(came)
    right, left = to_ep(own, 1, 0), to_ep(own, -1, 0)
    far = [to_ep(right[:160], 1, 0), to_ep(left[160:], -1, 0)]
    parts = call(
        expert_kernel,
        (shape(160, PIECE),) * 4,
        [SMEM] + [HBM] * 5 + [VMEM] * 6,
        scratch=[pltpu.VMEM((160, 2 * D), BF), pltpu.SemaphoreType.DMA((8,))],
        mib=16,
        flops=10 * 320 * 240 * D,
        bytes_accessed=18 * 10**6,
        name="expert",
    )(me, own, right, left, *far, *[in_vmem(w) for w in (*experts, *peers)])
    keep, give = sum_over_y(me, parts, "sum")
    back = call(expand_kernel, shape(256, CHUNK), [VMEM] * 2, name="expand")(keep, to_ep(give, 0, 1))
    back = lax.all_to_all(back.reshape(16, 16, CHUNK), "ctx", split_axis=0, concat_axis=0, tiled=True)

    stats, heads_out = call(
        stats_kernel,
        (shape(8, BLOCK, kind=F32), shape(2, HEAD_DIM, BLOCK, kind=F32)),
        [SMEM] + [VMEM] * 2,
        flops=4 * 2 * 2048 * 128 * 128,
        bytes_accessed=4 * 10**6,
        mib=16,
        name="stats",
    )(me, queries, gathered)

    back, stats, heads_out, dense_came = lax.optimization_barrier((back, stats, heads_out, to_ep(dense_give, 0, 1)))
    keep, give = call(
        combine_kernel,
        (shape(BLOCK, 256, kind=F32), shape(BLOCK, 256)),
        [SMEM] + [VMEM] * 4,
        name="combine",
    )(me, spots, back.reshape(256, CHUNK), dense_keep, dense_came)
    total = (keep + to_tp(give).astype(F32)).astype(BF)
    total = jnp.broadcast_to(total[None], (8, BLOCK, 256))
    total = lax.all_to_all(total, "ep", split_axis=0, concat_axis=0, tiled=True)
    grad_hidden, message = call(
        norm_kernel,
        (shape(BLOCK, D), shape(GRAY, 256)),
        [SMEM, VMEM, VMEM, VMEM, VMEM, VMEM, HBM, VMEM, VMEM],
        scratch=[pltpu.VMEM((BLOCK, D), BF), pltpu.VMEM((256, D), BF), pltpu.SemaphoreType.DMA((8,))],
        flops=4 * 128 * 256 * D,
        bytes_accessed=6 * 10**6,
        mib=16,
        name="norm",
    )(me, hidden, grad_out, gain, total, to_tp(total), in_hbm(out_proj), stats, heads_out)
    column = jnp.stack([message] + [to_ctx(message, -n, 0) for n in range(1, 4)])
    grad_q = call(
        queries_kernel,
        shape(BLOCK, 256),
        [SMEM] + [VMEM] * 3,
        scratch=[pltpu.VMEM((BLOCK, 256), F32)],
        flops=8 * 2 * 3 * 2 * 128**3,
        bytes_accessed=4 * 10**6,
        mib=16,
        name="queries",
    )(me, queries, gathered, message)

    def keys_part(shifts, columns, sums, first, last):
        return call(
            functools.partial(keys_kernel, shifts, first, last),
            (shape(BLOCK, 256, kind=BF if last else F32),) * 2,
            [SMEM] + [VMEM] * (1 + len(columns) + len(sums)),
            scratch=[pltpu.VMEM((BLOCK, 256), F32)] * 2,
            flops=4 * len(shifts) * 2 * 4 * 2 * 128**3,
            bytes_accessed=4 * 10**6,
            mib=16,
        name="keys",
        )(me, gathered, *columns, *sums)

    beside = [to_ctx(column, 0, -1), to_ctx(column, 0, 1)]
    opposite = to_ctx(column, 0, 2)
    sums = keys_part((0,), [column], [], True, False)
    sums = keys_part((1, 3), beside, sums, False, False)
    grad_k, grad_v = keys_part((2,), [opposite], sums, False, True)
    return grad_hidden, grad_q, grad_k, grad_v


def solution(mesh):
    return jax.shard_map(
        body,
        mesh=mesh,
        in_specs=(
            P("ctx", None),
            P("ctx", None),
            P(),
            P(("tp", "ep"), None),
            P(("tp", "ep"), None),
            P(("tp", "ep"), None),
            P("ctx", ("tp", "ep"), None),
            P("ctx", ("tp", "ep"), None),
            P("ctx", ("tp", "ep"), None),
            P(("tp", "ep"), None),
            P("ctx", ("tp", "ep")),
            P("ctx", ("tp", "ep")),
            P("ctx", ("tp", "ep")),
            P("ctx", None),
            P("ctx", None),
        ),
        out_specs=(
            P("ctx", None),
            P("ctx", ("tp", "ep")),
            P("ctx", ("tp", "ep")),
            P("ctx", ("tp", "ep")),
        ),
        check_vma=False,
    )
```

```python
import functools

import jax
import jax.numpy as jnp
from jax import lax
from jax.experimental import pallas as pl
from jax.experimental.pallas import tpu as pltpu
from jax.sharding import PartitionSpec as P

HEAD_DIM = 128
NEG_FILL = -1e30
EPSILON = 1e-05
BF = jnp.bfloat16
F32 = jnp.float32
BLOCK = 128
D = 3584
HALF = 10
PIECE = 896
CHUNK = 512
STRIDE = 24
SCALE = HEAD_DIM ** (-0.5)
CHUNKS = D // CHUNK
COLUMNS = [[4 * z + x for z in range(4)] for x in range(4)]
GRAY = 144
VMEM = pl.BlockSpec(memory_space=pltpu.VMEM)
SMEM = pl.BlockSpec(memory_space=pltpu.SMEM)
HBM = pl.BlockSpec(memory_space=pltpu.HBM)


def nt(a, b):
    return lax.dot_general(a, b, (((1,), (1,)), ((), ())), preferred_element_type=F32)


def tn(a, b):
    return lax.dot_general(a, b, (((0,), (0,)), ((), ())), preferred_element_type=F32)


def nn(a, b):
    return jnp.dot(a, b, preferred_element_type=F32)


def call(kernel, out_shape, in_specs, scratch=(), mib=12, flops=0, bytes_accessed=0, name=None):
    return pl.pallas_call(
        kernel,
        out_shape=out_shape,
        in_specs=in_specs,
        out_specs=jax.tree.map(lambda _: VMEM, out_shape),
        scratch_shapes=list(scratch),
        compiler_params=pltpu.CompilerParams(vmem_limit_bytes=mib * 1024 * 1024),
        cost_estimate=pl.CostEstimate(flops=flops, bytes_accessed=bytes_accessed, transcendentals=0),
        name=name,
    )


def in_hbm(x):
    return pltpu.with_memory_space_constraint(x, pltpu.HBM)


def to_tp(x):
    return lax.ppermute(x, "tp", [(0, 1), (1, 0)])


def to_ep(x, dy, dz):
    pairs = [(y * 2 + z, ((y + dy) % 4) * 2 + (z ^ dz)) for y in range(4) for z in range(2)]
    return lax.ppermute(x, "ep", pairs)


def to_ctx(x, dx):
    return lax.ppermute(x, "ctx", [(z * 4 + q, z * 4 + (q + dx) % 4) for z in range(4) for q in range(4)])


def sum_over_y(me, parts, name):
    size = shape(parts[0].shape[0], CHUNK)
    return call(sum_kernel, (size, size), [SMEM] + [VMEM] * 4, name=name)(
        me, parts[0], to_ep(parts[1], 1, 0), to_ep(parts[3], -1, 0), to_ep(parts[2], 2, 0)
    )


def prepare_kernel(
    me, hidden, grad_out, gain, ids, weights, queries, keys, values, mixed, send, spots, heads, hid_rows, grad_rows, sems
):
    copies = []
    for n in range(8):
        part = pl.ds(n * 16, 16)
        copies.append(pltpu.make_async_copy(hidden.at[part], hid_rows.at[part], sems.at[n]))
        copies[-1].start()
    lanes = pl.ds(pl.multiple_of((me[2] // 2 % 2) * 2 * PIECE, 2 * PIECE), 2 * PIECE)
    for n in range(4):
        part = pl.ds(n * 32, 32)
        copies.append(pltpu.make_async_copy(grad_out.at[part, lanes], grad_rows.at[part], sems.at[8 + n]))
        copies[-1].start()
    for n, source in enumerate((queries, keys, values)):
        copies.append(pltpu.make_async_copy(source, heads.at[:, pl.ds(n * 256, 256)], sems.at[12 + n]))
        copies[-1].start()
    tp = me[1]
    y = me[2] // 2
    experts = lax.broadcasted_iota(jnp.int32, (16, BLOCK), 0)
    hit = [(ids[k : k + 1, :] == experts).astype(F32) for k in range(2)]
    before = lax.broadcasted_iota(jnp.int32, (BLOCK, BLOCK), 0) < lax.broadcasted_iota(jnp.int32, (BLOCK, BLOCK), 1)
    earlier = nn((hit[0] + hit[1]).astype(BF), before.astype(BF))
    place_rows = lax.broadcasted_iota(jnp.int32, (256, BLOCK), 0)
    send_rows = lax.broadcasted_iota(jnp.int32, (16 * STRIDE, BLOCK), 0)
    spot = jnp.zeros((256, BLOCK), F32)
    own = [jnp.zeros((16 * STRIDE, BLOCK), F32) for _ in range(2)]
    weight = jnp.zeros((16 * STRIDE, BLOCK), F32)
    for k in range(2):
        slot = jnp.sum(earlier * hit[k], axis=0, keepdims=True).astype(jnp.int32)
        upper = (slot >= HALF).astype(jnp.int32)
        slot = slot - HALF * upper
        name = ids[k : k + 1, :]
        away = jnp.where(upper == tp, 0, 4096)
        spot = spot + (place_rows == name * 16 + slot + away).astype(F32)
        for h in range(2):
            mark = (send_rows == name * STRIDE + h * HALF + slot + away).astype(F32)
            own[h] = own[h] + mark
            weight = weight + mark * weights[k : k + 1, :]
    spots[...] = spot.astype(BF)
    scale = jnp.sum(weight, axis=1, keepdims=True)
    own = [o.astype(BF) for o in own]
    for n in range(8):
        copies[n].wait()
        part = slice(n * 16, (n + 1) * 16)
        hid = hid_rows[part, :].astype(F32)
        inverse = lax.rsqrt(jnp.mean(hid * hid, axis=1, keepdims=True) + EPSILON)
        mixed[part, :] = (hid * inverse * gain[...][None, :]).astype(BF)
    for copy in copies[8:]:
        copy.wait()

    @pl.when(y < 2)
    def _():
        at = (y % 2) * 2 * PIECE
        first = pl.ds(pl.multiple_of(at, PIECE), PIECE)
        second = pl.ds(pl.multiple_of(at + PIECE, PIECE), PIECE)
        rows = nn(own[0], mixed[:, first]) + nn(own[1], mixed[:, second])
        send[...] = rows.reshape(16, STRIDE, PIECE).astype(BF)

    @pl.when(y >= 2)
    def _():
        rows = (nn(own[0], grad_rows[:, :PIECE]) + nn(own[1], grad_rows[:, PIECE:])) * scale
        send[...] = rows.reshape(16, STRIDE, PIECE).astype(BF)


def compact_kernel(came, out):
    rows = came[...].astype(F32).reshape(16 * STRIDE, PIECE).astype(BF)
    to = lax.broadcasted_iota(jnp.int32, (320, 16 * STRIDE), 0)
    at = lax.broadcasted_iota(jnp.int32, (320, 16 * STRIDE), 1)
    block = at // STRIDE
    place = at - block * STRIDE
    half = (place >= HALF).astype(jnp.int32)
    pick = ((to == half * 160 + block * HALF + place - half * HALF) & (place < 2 * HALF)).astype(BF)
    out[...] = nn(pick, rows).astype(BF)


def gate_grads(a, b, back):
    s = jax.nn.sigmoid(a)
    ga = (back * b * s * (1.0 + a * (1.0 - s))).astype(BF)
    gb = (back * a * s).astype(BF)
    return ga, gb


def hidden_grads(x, y, gate, up, down):
    return gate_grads(nt(x, gate), nt(x, up), nt(y, down))


def piece_lanes(index):
    return pl.ds(pl.multiple_of(index * PIECE, PIECE), PIECE)


def dense_kernel(me, mixed, grad_out, gate_in, up_in, down_in, *refs):
    outs, (grad_rows, gate, up, down, sems) = refs[:4], refs[4:]
    copies = []
    for source, target in ((gate_in, gate), (up_in, up), (grad_out, grad_rows), (down_in, down)):
        for start in range(0, D, PIECE):
            part = pl.ds(start, PIECE)
            copies.append(pltpu.make_async_copy(source.at[:, part], target.at[:, part], sems.at[len(copies)]))
            copies[-1].start()
    for copy in copies[:4]:
        copy.wait()
    a = nt(mixed[...], gate[...])
    for copy in copies[4:8]:
        copy.wait()
    b = nt(mixed[...], up[...])
    for copy in copies[8:]:
        copy.wait()
    ga, gb = gate_grads(a, b, nt(grad_rows[...], down[...]))
    y = me[2] // 2
    for d, out in enumerate(outs):
        lanes = piece_lanes((y + d) % 4)
        out[...] = (nn(ga, gate[:, lanes]) + nn(gb, up[:, lanes])).astype(BF)


def load_kernel(*refs):
    count = (len(refs) - 1) // 2
    sems = refs[-1]
    copies = []
    for source, target in zip(refs[:count], refs[count:-1]):
        for n in range(3):
            part = pl.ds(n * 80, 80)
            copies.append(pltpu.make_async_copy(source.at[part], target.at[part], sems.at[len(copies)]))
            copies[-1].start()
    for copy in copies:
        copy.wait()


def expert_kernel(me, own, right, left, far0, far1, gate, up, down, gate2, up2, down2, *refs):
    outs, rows = refs[:4], refs[4]
    y = me[2] // 2
    for h in range(2):
        part = slice(h * 160, (h + 1) * 160)
        rows[:, piece_lanes(y * 2 + h)] = own[part, :]
        rows[:, piece_lanes((y + 3) % 4 * 2 + h)] = right[part, :]
        rows[:, piece_lanes((y + 1) % 4 * 2 + h)] = left[part, :]
    rows[:, piece_lanes((y + 2) % 4 * 2)] = far0[...]
    rows[:, piece_lanes((y + 2) % 4 * 2 + 1)] = far1[...]
    x, g = rows[:, :D], rows[:, D:]
    ga, gb = hidden_grads(x, g, gate[...], up[...], down[...])
    ga2, gb2 = hidden_grads(x, g, gate2[...], up2[...], down2[...])
    for d, out in enumerate(outs):
        lanes = piece_lanes((y + d) % 4)
        total = nn(ga, gate[:, lanes]) + nn(gb, up[:, lanes])
        total = total + (nn(ga2, gate2[:, lanes]) + nn(gb2, up2[:, lanes]))
        out[...] = total.astype(BF)


def sum_kernel(me, first, second, third, fourth, keep, give):
    z = me[2] % 2
    for side, out in ((z, keep), (1 - z, give)):
        lanes = pl.ds(pl.multiple_of(side * (PIECE - CHUNK), 128), CHUNK)
        total = first[:, lanes].astype(F32) + second[:, lanes].astype(F32)
        total = total + third[:, lanes].astype(F32) + fourth[:, lanes].astype(F32)
        out[...] = total.astype(BF)


def expand_kernel(keep, came, out):
    total = (keep[...].astype(F32) + came[...].astype(F32)).astype(BF)
    to = lax.broadcasted_iota(jnp.int32, (256, 160), 0)
    at = lax.broadcasted_iota(jnp.int32, (256, 160), 1)
    block = to // 16
    slot = to - block * 16
    pick = ((at == block * HALF + slot) & (slot < HALF)).astype(BF)
    out[...] = nn(pick, total).astype(BF)


def combine_kernel(me, spots, rows, dense_keep, dense_came, keep, give):
    tp = me[1]
    for half, out in ((tp, keep), (1 - tp, give)):
        lanes = pl.ds(pl.multiple_of(half * 256, 256), 256)
        total = tn(spots[...], rows[:, lanes]) + dense_keep[:, lanes].astype(F32) + dense_came[:, lanes].astype(F32)
        out[...] = total.astype(out.dtype)


def split3(x):
    hi = x.astype(BF).astype(F32)
    mid = (x - hi).astype(BF).astype(F32)
    return hi, mid, x - hi - mid


def norm_kernel(
    me, hidden, grad_out, gain, mine, other, proj_in, stats, heads_out, grad_hidden, message, total, out_proj, sems
):
    copies = []
    for n in range(8):
        part = pl.ds(n * 32, 32)
        copies.append(pltpu.make_async_copy(proj_in.at[part], out_proj.at[part], sems.at[n]))
        copies[-1].start()
    tp = me[1]
    for n in range(8):
        at = (n // 2) * PIECE + (n % 2) * (PIECE - CHUNK)
        total[:, pl.ds(pl.multiple_of(at + tp * 256, 128), 256)] = mine[n]
        total[:, pl.ds(pl.multiple_of(at + (1 - tp) * 256, 128), 256)] = other[n]
    hid = hidden[...].astype(F32)
    inverse = lax.rsqrt(jnp.mean(hid * hid, axis=1, keepdims=True) + EPSILON)
    normed = hid * inverse
    scaled = total[...].astype(F32) * gain[...][None, :]
    mean = jnp.mean(scaled * normed, axis=1, keepdims=True)
    grad = (grad_out[...].astype(F32) + inverse * (scaled - normed * mean)).astype(BF)
    grad_hidden[...] = grad
    for copy in copies:
        copy.wait()
    heads = nt(grad, out_proj[...]).astype(BF)
    rows = []
    for h in range(2):
        heads_t = jnp.transpose(heads[:, head(h)].astype(F32))
        delta = jnp.sum(heads_t * heads_out[h], axis=0, keepdims=True)
        rows.append(list(split3(stats[h : h + 1, :])) + list(split3(delta)))
    extra = jnp.concatenate(
        [jnp.concatenate([rows[0][k], rows[1][k]], axis=1) for k in range(6)] + [jnp.zeros((10, 256), F32)], axis=0
    ).astype(BF)
    for n in range(4):
        message[n, :BLOCK, :] = heads
        message[n, BLOCK:, :] = extra


def stats_kernel(me, own, gathered, stats, heads_out):
    block = me[0]
    key_at = lax.broadcasted_iota(jnp.int32, (2048, BLOCK), 0)
    query_at = lax.broadcasted_iota(jnp.int32, (2048, BLOCK), 1) + block * BLOCK
    allowed = key_at <= query_at
    lines = []
    for h in range(2):
        lanes = slice(h * HEAD_DIM, (h + 1) * HEAD_DIM)
        keys = gathered[:, 256 + h * HEAD_DIM : 256 + (h + 1) * HEAD_DIM]
        values = gathered[:, 512 + h * HEAD_DIM : 512 + (h + 1) * HEAD_DIM]
        scores = jnp.where(allowed, nt(keys, own[:, lanes]) * HEAD_DIM ** (-0.5), NEG_FILL)
        top = jnp.max(scores, axis=0, keepdims=True)
        weights = jnp.where(allowed, jnp.exp(scores - top), 0.0)
        lines.append(top + jnp.log(jnp.sum(weights, axis=0, keepdims=True)))
        half = weights.astype(BF)
        heads_out[h] = tn(values, half) / jnp.sum(half.astype(F32), axis=0, keepdims=True)
    stats[...] = jnp.concatenate(lines + [jnp.zeros((6, BLOCK), F32)], axis=0)


def pair(keys, values, queries, upstream, lines, allowed):
    log_norm = lines[0:1] + lines[1:2] + lines[2:3]
    delta = lines[3:4] + lines[4:5] + lines[5:6]
    probs = jnp.where(allowed, jnp.exp(nt(keys, queries) * SCALE - log_norm), 0.0)
    grad_scores = probs * (nt(values, upstream) - delta)
    return probs.astype(BF), grad_scores.astype(BF)


def head(h, start=0):
    return slice(start + h * HEAD_DIM, start + (h + 1) * HEAD_DIM)


def queries_kernel(me, own_q, gathered, grads, grad_q, total):
    block = me[0]
    message = grads.at[block // 4]
    lines = message[BLOCK:, :].astype(F32)
    query_at = lax.broadcasted_iota(jnp.int32, (512, BLOCK), 1) + block * BLOCK
    total[...] = jnp.zeros_like(total)
    for i in range(4):

        @pl.when(4 * i <= block)
        def _(i=i):
            rows = slice(i * 512, (i + 1) * 512)
            allowed = lax.broadcasted_iota(jnp.int32, (512, BLOCK), 0) + i * 512 <= query_at
            for h in range(2):
                keys = gathered[rows, head(h, 256)]
                values = gathered[rows, head(h, 512)]
                _, half = pair(keys, values, own_q[:, head(h)], message[:BLOCK, head(h)], lines[:, head(h)], allowed)
                total[:, head(h)] += tn(half, keys)

    grad_q[...] = (total[...] * SCALE).astype(BF)


def keys_kernel(shifts, first, last, me, gathered, *refs):
    count = len(shifts)
    grads, refs = refs[:count], refs[count:]
    if first:
        out_k, out_v, sum_k, sum_v = refs
        sum_k[...] = jnp.zeros_like(sum_k)
        sum_v[...] = jnp.zeros_like(sum_v)
    else:
        in_k, in_v, out_k, out_v, sum_k, sum_v = refs
        sum_k[...] = in_k[...]
        sum_v[...] = in_v[...]
    block = me[0]
    own_rows = pl.ds(pl.multiple_of(block * BLOCK, BLOCK), BLOCK)
    lane = lax.broadcasted_iota(jnp.int32, (BLOCK, 4 * BLOCK), 1)
    key_at = lax.broadcasted_iota(jnp.int32, (BLOCK, 4 * BLOCK), 0) + block * BLOCK
    for shift, source in zip(shifts, grads):
        column = (block + shift) % 4
        allowed = key_at <= (lane // BLOCK * 4 + column) * BLOCK + lane % BLOCK
        blocks = [n * 4 + column for n in range(4)]
        queries = jnp.concatenate(
            [gathered[pl.ds(pl.multiple_of(i * BLOCK, BLOCK), BLOCK), :256] for i in blocks], axis=0
        )
        upstream = jnp.concatenate([source[n, :BLOCK, :] for n in range(4)], axis=0)
        lines = [source[n, BLOCK:, :].astype(F32) for n in range(4)]
        for h in range(2):
            line = jnp.concatenate([part[:, head(h)] for part in lines], axis=1)
            keys = gathered[own_rows, head(h, 256)]
            values = gathered[own_rows, head(h, 512)]
            probs, half = pair(keys, values, queries[:, head(h)], upstream[:, head(h)], line, allowed)
            sum_k[:, head(h)] += nn(half, queries[:, head(h)])
            sum_v[:, head(h)] += nn(probs, upstream[:, head(h)])

    if last:
        out_k[...] = (sum_k[...] * SCALE).astype(BF)
        out_v[...] = sum_v[...].astype(BF)
    else:
        out_k[...] = sum_k[...]
        out_v[...] = sum_v[...]


def shape(*dims, kind=BF):
    return jax.ShapeDtypeStruct(dims, kind)


def body(
    hidden,
    grad_out,
    gain,
    dense_gate,
    dense_up,
    dense_down,
    expert_gate,
    expert_up,
    expert_down,
    out_proj,
    queries,
    keys,
    values,
    route_ids,
    route_weights,
):
    me = jnp.stack([lax.axis_index("ctx"), lax.axis_index("tp"), lax.axis_index("ep")]).astype(jnp.int32)
    experts = [expert_gate[0], expert_up[0], expert_down[0]]

    mixed, send, spots, heads = call(
        prepare_kernel,
        (shape(BLOCK, D), shape(16, STRIDE, PIECE), shape(256, BLOCK), shape(BLOCK, 768)),
        [SMEM, HBM, HBM, VMEM, VMEM, VMEM, HBM, HBM, HBM],
        scratch=[pltpu.VMEM((BLOCK, D), BF), pltpu.VMEM((BLOCK, 2 * PIECE), BF), pltpu.SemaphoreType.DMA((15,))],
        flops=10**8,
        bytes_accessed=4 * 10**6,
        mib=16,
        name="prepare",
    )(me, in_hbm(hidden), in_hbm(grad_out), gain, route_ids.T, route_weights.T, *[in_hbm(w) for w in (queries, keys, values)])
    gathered = lax.all_gather(heads, "ctx", axis=0, tiled=True)
    came = lax.all_to_all(send, "ctx", split_axis=0, concat_axis=0, tiled=True)

    dense = call(
        dense_kernel,
        (shape(BLOCK, PIECE),) * 4,
        [SMEM, VMEM] + [HBM] * 4,
        scratch=[pltpu.VMEM((BLOCK, D), BF)] + [pltpu.VMEM((152, D), BF)] * 3 + [pltpu.SemaphoreType.DMA((16,))],
        flops=10 * 128 * 152 * D,
        bytes_accessed=6 * 10**6,
        mib=16,
        name="dense",
    )(me, mixed, *[in_hbm(w) for w in (grad_out, dense_gate, dense_up, dense_down)])
    peers = [to_tp(w) for w in experts]
    dense_keep, dense_give = sum_over_y(me, dense, "dense_sum")

    came, dense_keep, dense_give = lax.optimization_barrier((came, dense_keep, dense_give))
    own = call(compact_kernel, shape(320, PIECE), [VMEM], name="compact")(came)
    right, left = to_ep(own, 1, 0), to_ep(own, -1, 0)
    far = [to_ep(right[:160], 1, 0), to_ep(left[160:], -1, 0)]
    *weights, _ = lax.optimization_barrier((*experts, *peers, own))
    weights = call(
        load_kernel,
        (shape(240, D),) * 6,
        [HBM] * 6,
        scratch=[pltpu.SemaphoreType.DMA((18,))],
        bytes_accessed=10**7,
        name="load",
    )(*[in_hbm(w) for w in weights])
    parts = call(
        expert_kernel,
        (shape(160, PIECE),) * 4,
        [SMEM] + [VMEM] * 11,
        scratch=[pltpu.VMEM((160, 2 * D), BF)],
        mib=16,
        flops=10 * 320 * 240 * D,
        bytes_accessed=18 * 10**6,
        name="expert",
    )(me, own, right, left, *far, *weights)
    keep, give = sum_over_y(me, parts, "sum")
    back = call(expand_kernel, shape(256, CHUNK), [VMEM] * 2, name="expand")(keep, to_ep(give, 0, 1))
    back = lax.all_to_all(back.reshape(16, 16, CHUNK), "ctx", split_axis=0, concat_axis=0, tiled=True)

    stats, heads_out = call(
        stats_kernel,
        (shape(8, BLOCK, kind=F32), shape(2, HEAD_DIM, BLOCK, kind=F32)),
        [SMEM] + [VMEM] * 2,
        flops=4 * 2 * 2048 * 128 * 128,
        bytes_accessed=4 * 10**6,
        mib=16,
        name="stats",
    )(me, queries, gathered)

    back, stats, heads_out, dense_came = lax.optimization_barrier((back, stats, heads_out, to_ep(dense_give, 0, 1)))
    keep, give = call(
        combine_kernel,
        (shape(BLOCK, 256, kind=F32), shape(BLOCK, 256)),
        [SMEM] + [VMEM] * 4,
        name="combine",
    )(me, spots, back.reshape(256, CHUNK), dense_keep, dense_came)
    total = (keep + to_tp(give).astype(F32)).astype(BF)
    total = jnp.broadcast_to(total[None], (8, BLOCK, 256))
    total = lax.all_to_all(total, "ep", split_axis=0, concat_axis=0, tiled=True)
    grad_hidden, message = call(
        norm_kernel,
        (shape(BLOCK, D), shape(4, GRAY, 256)),
        [SMEM, VMEM, VMEM, VMEM, VMEM, VMEM, HBM, VMEM, VMEM],
        scratch=[pltpu.VMEM((BLOCK, D), BF), pltpu.VMEM((256, D), BF), pltpu.SemaphoreType.DMA((8,))],
        flops=4 * 128 * 256 * D,
        bytes_accessed=6 * 10**6,
        mib=16,
        name="norm",
    )(me, hidden, grad_out, gain, total, to_tp(total), in_hbm(out_proj), stats, heads_out)
    column = lax.all_to_all(message, "ctx", split_axis=0, concat_axis=0, tiled=True, axis_index_groups=COLUMNS)
    grad_q = call(
        queries_kernel,
        shape(BLOCK, 256),
        [SMEM] + [VMEM] * 3,
        scratch=[pltpu.VMEM((BLOCK, 256), F32)],
        flops=8 * 2 * 3 * 2 * 128**3,
        bytes_accessed=4 * 10**6,
        mib=16,
        name="queries",
    )(me, queries, gathered, column)

    def keys_part(shifts, columns, sums, first, last):
        return call(
            functools.partial(keys_kernel, shifts, first, last),
            (shape(BLOCK, 256, kind=BF if last else F32),) * 2,
            [SMEM] + [VMEM] * (1 + len(columns) + len(sums)),
            scratch=[pltpu.VMEM((BLOCK, 256), F32)] * 2,
            flops=4 * len(shifts) * 2 * 4 * 2 * 128**3,
            bytes_accessed=4 * 10**6,
            mib=16,
        name="keys",
        )(me, gathered, *columns, *sums)

    beside = [to_ctx(column, -1), to_ctx(column, 1)]
    opposite = to_ctx(column, 2)
    sums = keys_part((0,), [column], [], True, False)
    sums = keys_part((1, 3), beside, sums, False, False)
    grad_k, grad_v = keys_part((2,), [opposite], sums, False, True)
    return grad_hidden, grad_q, grad_k, grad_v


def solution(mesh):
    return jax.shard_map(
        body,
        mesh=mesh,
        in_specs=(
            P("ctx", None),
            P("ctx", None),
            P(),
            P(("tp", "ep"), None),
            P(("tp", "ep"), None),
            P(("tp", "ep"), None),
            P("ctx", ("tp", "ep"), None),
            P("ctx", ("tp", "ep"), None),
            P("ctx", ("tp", "ep"), None),
            P(("tp", "ep"), None),
            P("ctx", ("tp", "ep")),
            P("ctx", ("tp", "ep")),
            P("ctx", ("tp", "ep")),
            P("ctx", None),
            P("ctx", None),
        ),
        out_specs=(
            P("ctx", None),
            P("ctx", ("tp", "ep")),
            P("ctx", ("tp", "ep")),
            P("ctx", ("tp", "ep")),
        ),
        check_vma=False,
    )
```

```python
import functools

import jax
import jax.numpy as jnp
from jax import lax
from jax.experimental import pallas as pl
from jax.experimental.pallas import tpu as pltpu
from jax.sharding import PartitionSpec as P

HEAD_DIM = 128
NEG_FILL = -1e30
EPSILON = 1e-05
BF = jnp.bfloat16
F32 = jnp.float32
BLOCK = 128
D = 3584
HALF = 10
PIECE = 896
CHUNK = 512
STRIDE = 24
SCALE = HEAD_DIM ** (-0.5)
CHUNKS = D // CHUNK
COLUMNS = [[4 * z + x for z in range(4)] for x in range(4)]
GRAY = 144
VMEM = pl.BlockSpec(memory_space=pltpu.VMEM)
SMEM = pl.BlockSpec(memory_space=pltpu.SMEM)
HBM = pl.BlockSpec(memory_space=pltpu.HBM)


def nt(a, b):
    return lax.dot_general(a, b, (((1,), (1,)), ((), ())), preferred_element_type=F32)


def tn(a, b):
    return lax.dot_general(a, b, (((0,), (0,)), ((), ())), preferred_element_type=F32)


def nn(a, b):
    return jnp.dot(a, b, preferred_element_type=F32)


def call(kernel, out_shape, in_specs, scratch=(), mib=12, flops=0, bytes_accessed=0, name=None):
    return pl.pallas_call(
        kernel,
        out_shape=out_shape,
        in_specs=in_specs,
        out_specs=jax.tree.map(lambda _: VMEM, out_shape),
        scratch_shapes=list(scratch),
        compiler_params=pltpu.CompilerParams(vmem_limit_bytes=mib * 1024 * 1024),
        cost_estimate=pl.CostEstimate(flops=flops, bytes_accessed=bytes_accessed, transcendentals=0),
        name=name,
    )


def in_hbm(x):
    return pltpu.with_memory_space_constraint(x, pltpu.HBM)


def to_tp(x):
    return lax.ppermute(x, "tp", [(0, 1), (1, 0)])


def to_ep(x, dy, dz):
    pairs = [(y * 2 + z, ((y + dy) % 4) * 2 + (z ^ dz)) for y in range(4) for z in range(2)]
    return lax.ppermute(x, "ep", pairs)


def to_ctx(x, dx):
    return lax.ppermute(x, "ctx", [(z * 4 + q, z * 4 + (q + dx) % 4) for z in range(4) for q in range(4)])


def sum_over_y(me, parts, name):
    size = shape(parts[0].shape[0], CHUNK)
    return call(sum_kernel, (size, size), [SMEM] + [VMEM] * 4, name=name)(
        me, parts[0], to_ep(parts[1], 1, 0), to_ep(parts[3], -1, 0), to_ep(parts[2], 2, 0)
    )


def prepare_kernel(
    me, hidden, grad_out, gain, ids, weights, queries, keys, values, mixed, send, spots, heads, hid_rows, grad_rows, sems
):
    copies = []
    for n in range(8):
        part = pl.ds(n * 16, 16)
        copies.append(pltpu.make_async_copy(hidden.at[part], hid_rows.at[part], sems.at[n]))
        copies[-1].start()
    lanes = pl.ds(pl.multiple_of((me[2] // 2 % 2) * 2 * PIECE, 2 * PIECE), 2 * PIECE)
    for n in range(4):
        part = pl.ds(n * 32, 32)
        copies.append(pltpu.make_async_copy(grad_out.at[part, lanes], grad_rows.at[part], sems.at[8 + n]))
        copies[-1].start()
    for n, source in enumerate((queries, keys, values)):
        copies.append(pltpu.make_async_copy(source, heads.at[:, pl.ds(n * 256, 256)], sems.at[12 + n]))
        copies[-1].start()
    tp = me[1]
    y = me[2] // 2
    experts = lax.broadcasted_iota(jnp.int32, (16, BLOCK), 0)
    hit = [(ids[k : k + 1, :] == experts).astype(F32) for k in range(2)]
    before = lax.broadcasted_iota(jnp.int32, (BLOCK, BLOCK), 0) < lax.broadcasted_iota(jnp.int32, (BLOCK, BLOCK), 1)
    earlier = nn((hit[0] + hit[1]).astype(BF), before.astype(BF))
    place_rows = lax.broadcasted_iota(jnp.int32, (256, BLOCK), 0)
    send_rows = lax.broadcasted_iota(jnp.int32, (16 * STRIDE, BLOCK), 0)
    spot = jnp.zeros((256, BLOCK), F32)
    own = [jnp.zeros((16 * STRIDE, BLOCK), F32) for _ in range(2)]
    weight = jnp.zeros((16 * STRIDE, BLOCK), F32)
    for k in range(2):
        slot = jnp.sum(earlier * hit[k], axis=0, keepdims=True).astype(jnp.int32)
        upper = (slot >= HALF).astype(jnp.int32)
        slot = slot - HALF * upper
        name = ids[k : k + 1, :]
        away = jnp.where(upper == tp, 0, 4096)
        spot = spot + (place_rows == name * 16 + slot + away).astype(F32)
        for h in range(2):
            mark = (send_rows == name * STRIDE + h * HALF + slot + away).astype(F32)
            own[h] = own[h] + mark
            weight = weight + mark * weights[k : k + 1, :]
    spots[...] = spot.astype(BF)
    scale = jnp.sum(weight, axis=1, keepdims=True)
    own = [o.astype(BF) for o in own]
    for n in range(8):
        copies[n].wait()
        part = slice(n * 16, (n + 1) * 16)
        hid = hid_rows[part, :].astype(F32)
        inverse = lax.rsqrt(jnp.mean(hid * hid, axis=1, keepdims=True) + EPSILON)
        mixed[part, :] = (hid * inverse * gain[...][None, :]).astype(BF)
    for copy in copies[8:]:
        copy.wait()

    @pl.when(y < 2)
    def _():
        at = (y % 2) * 2 * PIECE
        first = pl.ds(pl.multiple_of(at, PIECE), PIECE)
        second = pl.ds(pl.multiple_of(at + PIECE, PIECE), PIECE)
        rows = nn(own[0], mixed[:, first]) + nn(own[1], mixed[:, second])
        send[...] = rows.reshape(16, STRIDE, PIECE).astype(BF)

    @pl.when(y >= 2)
    def _():
        rows = (nn(own[0], grad_rows[:, :PIECE]) + nn(own[1], grad_rows[:, PIECE:])) * scale
        send[...] = rows.reshape(16, STRIDE, PIECE).astype(BF)


def compact_kernel(came, out):
    rows = came[...].astype(F32).reshape(16 * STRIDE, PIECE).astype(BF)
    to = lax.broadcasted_iota(jnp.int32, (320, 16 * STRIDE), 0)
    at = lax.broadcasted_iota(jnp.int32, (320, 16 * STRIDE), 1)
    block = at // STRIDE
    place = at - block * STRIDE
    half = (place >= HALF).astype(jnp.int32)
    pick = ((to == half * 160 + block * HALF + place - half * HALF) & (place < 2 * HALF)).astype(BF)
    out[...] = nn(pick, rows).astype(BF)


def gate_grads(a, b, back):
    s = jax.nn.sigmoid(a)
    ga = (back * b * s * (1.0 + a * (1.0 - s))).astype(BF)
    gb = (back * a * s).astype(BF)
    return ga, gb


def hidden_grads(x, y, gate, up, down):
    return gate_grads(nt(x, gate), nt(x, up), nt(y, down))


def piece_lanes(index):
    return pl.ds(pl.multiple_of(index * PIECE, PIECE), PIECE)


def dense_kernel(me, mixed, grad_out, gate_in, up_in, down_in, *refs):
    outs, (grad_rows, gate, up, down, sems) = refs[:4], refs[4:]
    copies = []
    for source, target in ((gate_in, gate), (up_in, up), (grad_out, grad_rows), (down_in, down)):
        for start in range(0, D, PIECE):
            part = pl.ds(start, PIECE)
            copies.append(pltpu.make_async_copy(source.at[:, part], target.at[:, part], sems.at[len(copies)]))
            copies[-1].start()
    for copy in copies[:4]:
        copy.wait()
    a = nt(mixed[...], gate[...])
    for copy in copies[4:8]:
        copy.wait()
    b = nt(mixed[...], up[...])
    for copy in copies[8:]:
        copy.wait()
    ga, gb = gate_grads(a, b, nt(grad_rows[...], down[...]))
    y = me[2] // 2
    for d, out in enumerate(outs):
        lanes = piece_lanes((y + d) % 4)
        out[...] = (nn(ga, gate[:, lanes]) + nn(gb, up[:, lanes])).astype(BF)


def load_kernel(*refs):
    count = (len(refs) - 1) // 2
    sems = refs[-1]
    copies = []
    for source, target in zip(refs[:count], refs[count:-1]):
        for n in range(3):
            part = pl.ds(n * 80, 80)
            copies.append(pltpu.make_async_copy(source.at[part], target.at[part], sems.at[len(copies)]))
            copies[-1].start()
    for copy in copies:
        copy.wait()


def expert_kernel(me, own, right, left, far0, far1, gate, up, down, gate2, up2, down2, *refs):
    outs, rows = refs[:4], refs[4]
    y = me[2] // 2
    for h in range(2):
        part = slice(h * 160, (h + 1) * 160)
        rows[:, piece_lanes(y * 2 + h)] = own[part, :]
        rows[:, piece_lanes((y + 3) % 4 * 2 + h)] = right[part, :]
        rows[:, piece_lanes((y + 1) % 4 * 2 + h)] = left[part, :]
    rows[:, piece_lanes((y + 2) % 4 * 2)] = far0[...]
    rows[:, piece_lanes((y + 2) % 4 * 2 + 1)] = far1[...]
    x, g = rows[:, :D], rows[:, D:]
    ga, gb = hidden_grads(x, g, gate[...], up[...], down[...])
    ga2, gb2 = hidden_grads(x, g, gate2[...], up2[...], down2[...])
    for d, out in enumerate(outs):
        lanes = piece_lanes((y + d) % 4)
        total = nn(ga, gate[:, lanes]) + nn(gb, up[:, lanes])
        total = total + (nn(ga2, gate2[:, lanes]) + nn(gb2, up2[:, lanes]))
        out[...] = total.astype(BF)


def sum_kernel(me, first, second, third, fourth, keep, give):
    z = me[2] % 2
    for side, out in ((z, keep), (1 - z, give)):
        lanes = pl.ds(pl.multiple_of(side * (PIECE - CHUNK), 128), CHUNK)
        total = first[:, lanes].astype(F32) + second[:, lanes].astype(F32)
        total = total + third[:, lanes].astype(F32) + fourth[:, lanes].astype(F32)
        out[...] = total.astype(BF)


def expand_kernel(keep, came, out):
    total = (keep[...].astype(F32) + came[...].astype(F32)).astype(BF)
    to = lax.broadcasted_iota(jnp.int32, (256, 160), 0)
    at = lax.broadcasted_iota(jnp.int32, (256, 160), 1)
    block = to // 16
    slot = to - block * 16
    pick = ((at == block * HALF + slot) & (slot < HALF)).astype(BF)
    out[...] = nn(pick, total).astype(BF)


def combine_kernel(me, spots, rows, dense_keep, dense_came, keep, give):
    tp = me[1]
    for half, out in ((tp, keep), (1 - tp, give)):
        lanes = pl.ds(pl.multiple_of(half * 256, 256), 256)
        total = tn(spots[...], rows[:, lanes]) + dense_keep[:, lanes].astype(F32) + dense_came[:, lanes].astype(F32)
        out[...] = total.astype(out.dtype)


def split3(x):
    hi = x.astype(BF).astype(F32)
    mid = (x - hi).astype(BF).astype(F32)
    return hi, mid, x - hi - mid


def norm_kernel(
    me, hidden, grad_out, gain, mine, other, proj_in, stats, heads_out, grad_hidden, message, total, out_proj, sems
):
    copies = []
    for n in range(8):
        part = pl.ds(n * 32, 32)
        copies.append(pltpu.make_async_copy(proj_in.at[part], out_proj.at[part], sems.at[n]))
        copies[-1].start()
    tp = me[1]
    for n in range(8):
        at = (n // 2) * PIECE + (n % 2) * (PIECE - CHUNK)
        total[:, pl.ds(pl.multiple_of(at + tp * 256, 128), 256)] = mine[n]
        total[:, pl.ds(pl.multiple_of(at + (1 - tp) * 256, 128), 256)] = other[n]
    hid = hidden[...].astype(F32)
    inverse = lax.rsqrt(jnp.mean(hid * hid, axis=1, keepdims=True) + EPSILON)
    normed = hid * inverse
    scaled = total[...].astype(F32) * gain[...][None, :]
    mean = jnp.mean(scaled * normed, axis=1, keepdims=True)
    grad = (grad_out[...].astype(F32) + inverse * (scaled - normed * mean)).astype(BF)
    grad_hidden[...] = grad
    for copy in copies:
        copy.wait()
    heads = nt(grad, out_proj[...]).astype(BF)
    rows = []
    for h in range(2):
        heads_t = jnp.transpose(heads[:, head(h)].astype(F32))
        delta = jnp.sum(heads_t * heads_out[h], axis=0, keepdims=True)
        rows.append(list(split3(stats[h : h + 1, :])) + list(split3(delta)))
    extra = jnp.concatenate(
        [jnp.concatenate([rows[0][k], rows[1][k]], axis=1) for k in range(6)] + [jnp.zeros((10, 256), F32)], axis=0
    ).astype(BF)
    for n in range(4):
        message[n, :BLOCK, :] = heads
        message[n, BLOCK:, :] = extra


def stats_kernel(me, own, gathered, stats, heads_out):
    block = me[0]
    key_at = lax.broadcasted_iota(jnp.int32, (2048, BLOCK), 0)
    query_at = lax.broadcasted_iota(jnp.int32, (2048, BLOCK), 1) + block * BLOCK
    allowed = key_at <= query_at
    lines = []
    for h in range(2):
        lanes = slice(h * HEAD_DIM, (h + 1) * HEAD_DIM)
        keys = gathered[:, 256 + h * HEAD_DIM : 256 + (h + 1) * HEAD_DIM]
        values = gathered[:, 512 + h * HEAD_DIM : 512 + (h + 1) * HEAD_DIM]
        scores = jnp.where(allowed, nt(keys, own[:, lanes]) * HEAD_DIM ** (-0.5), NEG_FILL)
        top = jnp.max(scores, axis=0, keepdims=True)
        weights = jnp.where(allowed, jnp.exp(scores - top), 0.0)
        lines.append(top + jnp.log(jnp.sum(weights, axis=0, keepdims=True)))
        half = weights.astype(BF)
        heads_out[h] = tn(values, half) / jnp.sum(half.astype(F32), axis=0, keepdims=True)
    stats[...] = jnp.concatenate(lines + [jnp.zeros((6, BLOCK), F32)], axis=0)


def pair(keys, values, queries, upstream, lines, allowed):
    log_norm = lines[0:1] + lines[1:2] + lines[2:3]
    delta = lines[3:4] + lines[4:5] + lines[5:6]
    probs = jnp.where(allowed, jnp.exp(nt(keys, queries) * SCALE - log_norm), 0.0)
    grad_scores = probs * (nt(values, upstream) - delta)
    return probs.astype(BF), grad_scores.astype(BF)


def head(h, start=0):
    return slice(start + h * HEAD_DIM, start + (h + 1) * HEAD_DIM)


def queries_kernel(me, own_q, gathered, grads, grad_q, total):
    block = me[0]
    message = grads.at[block // 4]
    lines = message[BLOCK:, :].astype(F32)
    query_at = lax.broadcasted_iota(jnp.int32, (512, BLOCK), 1) + block * BLOCK
    total[...] = jnp.zeros_like(total)
    for i in range(4):

        @pl.when(4 * i <= block)
        def _(i=i):
            rows = slice(i * 512, (i + 1) * 512)
            allowed = lax.broadcasted_iota(jnp.int32, (512, BLOCK), 0) + i * 512 <= query_at
            for h in range(2):
                keys = gathered[rows, head(h, 256)]
                values = gathered[rows, head(h, 512)]
                _, half = pair(keys, values, own_q[:, head(h)], message[:BLOCK, head(h)], lines[:, head(h)], allowed)
                total[:, head(h)] += tn(half, keys)

    grad_q[...] = (total[...] * SCALE).astype(BF)


def keys_kernel(shifts, first, last, me, gathered, *refs):
    count = len(shifts)
    grads, refs = refs[:count], refs[count:]
    if first:
        out_k, out_v, sum_k, sum_v = refs
        sum_k[...] = jnp.zeros_like(sum_k)
        sum_v[...] = jnp.zeros_like(sum_v)
    else:
        in_k, in_v, out_k, out_v, sum_k, sum_v = refs
        sum_k[...] = in_k[...]
        sum_v[...] = in_v[...]
    block = me[0]
    own_rows = pl.ds(pl.multiple_of(block * BLOCK, BLOCK), BLOCK)
    lane = lax.broadcasted_iota(jnp.int32, (BLOCK, 4 * BLOCK), 1)
    key_at = lax.broadcasted_iota(jnp.int32, (BLOCK, 4 * BLOCK), 0) + block * BLOCK
    for shift, source in zip(shifts, grads):
        column = (block + shift) % 4
        allowed = key_at <= (lane // BLOCK * 4 + column) * BLOCK + lane % BLOCK
        blocks = [n * 4 + column for n in range(4)]
        queries = jnp.concatenate(
            [gathered[pl.ds(pl.multiple_of(i * BLOCK, BLOCK), BLOCK), :256] for i in blocks], axis=0
        )
        upstream = jnp.concatenate([source[n, :BLOCK, :] for n in range(4)], axis=0)
        lines = [source[n, BLOCK:, :].astype(F32) for n in range(4)]
        for h in range(2):
            line = jnp.concatenate([part[:, head(h)] for part in lines], axis=1)
            keys = gathered[own_rows, head(h, 256)]
            values = gathered[own_rows, head(h, 512)]
            probs, half = pair(keys, values, queries[:, head(h)], upstream[:, head(h)], line, allowed)
            sum_k[:, head(h)] += nn(half, queries[:, head(h)])
            sum_v[:, head(h)] += nn(probs, upstream[:, head(h)])

    if last:
        out_k[...] = (sum_k[...] * SCALE).astype(BF)
        out_v[...] = sum_v[...].astype(BF)
    else:
        out_k[...] = sum_k[...]
        out_v[...] = sum_v[...]


def shape(*dims, kind=BF):
    return jax.ShapeDtypeStruct(dims, kind)


def body(
    hidden,
    grad_out,
    gain,
    dense_gate,
    dense_up,
    dense_down,
    expert_gate,
    expert_up,
    expert_down,
    out_proj,
    queries,
    keys,
    values,
    route_ids,
    route_weights,
):
    me = jnp.stack([lax.axis_index("ctx"), lax.axis_index("tp"), lax.axis_index("ep")]).astype(jnp.int32)
    experts = [expert_gate[0], expert_up[0], expert_down[0]]

    mixed, send, spots, heads = call(
        prepare_kernel,
        (shape(BLOCK, D), shape(16, STRIDE, PIECE), shape(256, BLOCK), shape(BLOCK, 768)),
        [SMEM, HBM, HBM, VMEM, VMEM, VMEM, HBM, HBM, HBM],
        scratch=[pltpu.VMEM((BLOCK, D), BF), pltpu.VMEM((BLOCK, 2 * PIECE), BF), pltpu.SemaphoreType.DMA((15,))],
        flops=10**8,
        bytes_accessed=4 * 10**6,
        mib=16,
        name="prepare",
    )(me, in_hbm(hidden), in_hbm(grad_out), gain, route_ids.T, route_weights.T, *[in_hbm(w) for w in (queries, keys, values)])
    gathered = lax.all_gather(heads, "ctx", axis=0, tiled=True)
    came = lax.all_to_all(send, "ctx", split_axis=0, concat_axis=0, tiled=True)

    dense = call(
        dense_kernel,
        (shape(BLOCK, PIECE),) * 4,
        [SMEM, VMEM] + [HBM] * 4,
        scratch=[pltpu.VMEM((BLOCK, D), BF)] + [pltpu.VMEM((152, D), BF)] * 3 + [pltpu.SemaphoreType.DMA((16,))],
        flops=10 * 128 * 152 * D,
        bytes_accessed=6 * 10**6,
        mib=16,
        name="dense",
    )(me, mixed, *[in_hbm(w) for w in (grad_out, dense_gate, dense_up, dense_down)])
    peers = [to_tp(w) for w in experts]
    dense_keep, dense_give = sum_over_y(me, dense, "dense_sum")

    came, dense_keep, dense_give = lax.optimization_barrier((came, dense_keep, dense_give))
    own = call(compact_kernel, shape(320, PIECE), [VMEM], name="compact")(came)
    right, left = to_ep(own, 1, 0), to_ep(own, -1, 0)
    far = [to_ep(right[:160], 1, 0), to_ep(left[160:], -1, 0)]
    *weights, _ = lax.optimization_barrier((*experts, *peers, own))
    weights = call(
        load_kernel,
        (shape(240, D),) * 6,
        [HBM] * 6,
        scratch=[pltpu.SemaphoreType.DMA((18,))],
        bytes_accessed=10**7,
        name="load",
    )(*[in_hbm(w) for w in weights])
    parts = call(
        expert_kernel,
        (shape(160, PIECE),) * 4,
        [SMEM] + [VMEM] * 11,
        scratch=[pltpu.VMEM((160, 2 * D), BF)],
        mib=16,
        flops=10 * 320 * 240 * D,
        bytes_accessed=18 * 10**6,
        name="expert",
    )(me, own, right, left, *far, *weights)
    keep, give = sum_over_y(me, parts, "sum")
    back = call(expand_kernel, shape(256, CHUNK), [VMEM] * 2, name="expand")(keep, to_ep(give, 0, 1))
    back = lax.all_to_all(back.reshape(16, 16, CHUNK), "ctx", split_axis=0, concat_axis=0, tiled=True)

    stats, heads_out = call(
        stats_kernel,
        (shape(8, BLOCK, kind=F32), shape(2, HEAD_DIM, BLOCK, kind=F32)),
        [SMEM] + [VMEM] * 2,
        flops=4 * 2 * 2048 * 128 * 128,
        bytes_accessed=4 * 10**6,
        mib=16,
        name="stats",
    )(me, queries, gathered)

    back, stats, heads_out, dense_came = lax.optimization_barrier((back, stats, heads_out, to_ep(dense_give, 0, 1)))
    keep, give = call(
        combine_kernel,
        (shape(BLOCK, 256, kind=F32), shape(BLOCK, 256)),
        [SMEM] + [VMEM] * 4,
        name="combine",
    )(me, spots, back.reshape(256, CHUNK), dense_keep, dense_came)
    total = (keep + to_tp(give).astype(F32)).astype(BF)
    total = jnp.broadcast_to(total[None], (8, BLOCK, 256))
    total = lax.all_to_all(total, "ep", split_axis=0, concat_axis=0, tiled=True)
    grad_hidden, message = call(
        norm_kernel,
        (shape(BLOCK, D), shape(4, GRAY, 256)),
        [SMEM, VMEM, VMEM, VMEM, VMEM, VMEM, HBM, VMEM, VMEM],
        scratch=[pltpu.VMEM((BLOCK, D), BF), pltpu.VMEM((256, D), BF), pltpu.SemaphoreType.DMA((8,))],
        flops=4 * 128 * 256 * D,
        bytes_accessed=6 * 10**6,
        mib=16,
        name="norm",
    )(me, hidden, grad_out, gain, total, to_tp(total), in_hbm(out_proj), stats, heads_out)
    column = lax.all_to_all(message, "ctx", split_axis=0, concat_axis=0, tiled=True, axis_index_groups=COLUMNS)
    grad_q = call(
        queries_kernel,
        shape(BLOCK, 256),
        [SMEM] + [VMEM] * 3,
        scratch=[pltpu.VMEM((BLOCK, 256), F32)],
        flops=8 * 2 * 3 * 2 * 128**3,
        bytes_accessed=4 * 10**6,
        mib=16,
        name="queries",
    )(me, queries, gathered, column)

    def keys_part(shifts, columns, sums, first, last):
        return call(
            functools.partial(keys_kernel, shifts, first, last),
            (shape(BLOCK, 256, kind=BF if last else F32),) * 2,
            [SMEM] + [VMEM] * (1 + len(columns) + len(sums)),
            scratch=[pltpu.VMEM((BLOCK, 256), F32)] * 2,
            flops=4 * len(shifts) * 2 * 4 * 2 * 128**3,
            bytes_accessed=4 * 10**6,
            mib=16,
        name="keys",
        )(me, gathered, *columns, *sums)

    opposite = to_ctx(column, 2)
    beside = [to_ctx(column, -1), to_ctx(column, 1)]
    sums = keys_part((0,), [column], [], True, False)
    sums = keys_part((2,), [opposite], sums, False, False)
    grad_k, grad_v = keys_part((1, 3), beside, sums, False, True)
    return grad_hidden, grad_q, grad_k, grad_v


def solution(mesh):
    return jax.shard_map(
        body,
        mesh=mesh,
        in_specs=(
            P("ctx", None),
            P("ctx", None),
            P(),
            P(("tp", "ep"), None),
            P(("tp", "ep"), None),
            P(("tp", "ep"), None),
            P("ctx", ("tp", "ep"), None),
            P("ctx", ("tp", "ep"), None),
            P("ctx", ("tp", "ep"), None),
            P(("tp", "ep"), None),
            P("ctx", ("tp", "ep")),
            P("ctx", ("tp", "ep")),
            P("ctx", ("tp", "ep")),
            P("ctx", None),
            P("ctx", None),
        ),
        out_specs=(
            P("ctx", None),
            P("ctx", ("tp", "ep")),
            P("ctx", ("tp", "ep")),
            P("ctx", ("tp", "ep")),
        ),
        check_vma=False,
    )
```

```python
import functools

import jax
import jax.numpy as jnp
from jax import lax
from jax.experimental import pallas as pl
from jax.experimental.pallas import tpu as pltpu
from jax.sharding import PartitionSpec as P

HEAD_DIM = 128
NEG_FILL = -1e30
EPSILON = 1e-05
BF = jnp.bfloat16
F32 = jnp.float32
BLOCK = 128
D = 3584
HALF = 10
PIECE = 896
CHUNK = 512
STRIDE = 24
SCALE = HEAD_DIM ** (-0.5)
CHUNKS = D // CHUNK
COLUMNS = [[4 * z + x for z in range(4)] for x in range(4)]
GRAY = 144
VMEM = pl.BlockSpec(memory_space=pltpu.VMEM)
SMEM = pl.BlockSpec(memory_space=pltpu.SMEM)
HBM = pl.BlockSpec(memory_space=pltpu.HBM)


def nt(a, b):
    return lax.dot_general(a, b, (((1,), (1,)), ((), ())), preferred_element_type=F32)


def tn(a, b):
    return lax.dot_general(a, b, (((0,), (0,)), ((), ())), preferred_element_type=F32)


def nn(a, b):
    return jnp.dot(a, b, preferred_element_type=F32)


def call(kernel, out_shape, in_specs, scratch=(), mib=12, flops=0, bytes_accessed=0, name=None):
    return pl.pallas_call(
        kernel,
        out_shape=out_shape,
        in_specs=in_specs,
        out_specs=jax.tree.map(lambda _: VMEM, out_shape),
        scratch_shapes=list(scratch),
        compiler_params=pltpu.CompilerParams(vmem_limit_bytes=mib * 1024 * 1024),
        cost_estimate=pl.CostEstimate(flops=flops, bytes_accessed=bytes_accessed, transcendentals=0),
        name=name,
    )


def in_hbm(x):
    return pltpu.with_memory_space_constraint(x, pltpu.HBM)


def to_tp(x):
    return lax.ppermute(x, "tp", [(0, 1), (1, 0)])


def to_ep(x, dy, dz):
    pairs = [(y * 2 + z, ((y + dy) % 4) * 2 + (z ^ dz)) for y in range(4) for z in range(2)]
    return lax.ppermute(x, "ep", pairs)


def to_ctx(x, dx):
    return lax.ppermute(x, "ctx", [(z * 4 + q, z * 4 + (q + dx) % 4) for z in range(4) for q in range(4)])


def sum_over_y(me, parts, name):
    size = shape(parts[0].shape[0], CHUNK)
    order = ((2, 2), (1, 1), (3, -1)) if name == "dense_sum" else ((1, 1), (3, -1), (2, 2))
    moved = [to_ep(parts[n], dy, 0) for n, dy in order]
    return call(sum_kernel, (size, size), [SMEM] + [VMEM] * 4, name=name)(
        me, parts[0], *moved
    )


def prepare_kernel(
    me, hidden, grad_out, gain, ids, weights, queries, keys, values, mixed, send, spots, heads, hid_rows, grad_rows, sems
):
    copies = []
    for n in range(8):
        part = pl.ds(n * 16, 16)
        copies.append(pltpu.make_async_copy(hidden.at[part], hid_rows.at[part], sems.at[n]))
        copies[-1].start()
    lanes = pl.ds(pl.multiple_of((me[2] // 2 % 2) * 2 * PIECE, 2 * PIECE), 2 * PIECE)
    for n in range(4):
        part = pl.ds(n * 32, 32)
        copies.append(pltpu.make_async_copy(grad_out.at[part, lanes], grad_rows.at[part], sems.at[8 + n]))
        copies[-1].start()
    for n, source in enumerate((queries, keys, values)):
        copies.append(pltpu.make_async_copy(source, heads.at[:, pl.ds(n * 256, 256)], sems.at[12 + n]))
        copies[-1].start()
    tp = me[1]
    y = me[2] // 2
    experts = lax.broadcasted_iota(jnp.int32, (16, BLOCK), 0)
    hit = [(ids[k : k + 1, :] == experts).astype(F32) for k in range(2)]
    before = lax.broadcasted_iota(jnp.int32, (BLOCK, BLOCK), 0) < lax.broadcasted_iota(jnp.int32, (BLOCK, BLOCK), 1)
    earlier = nn((hit[0] + hit[1]).astype(BF), before.astype(BF))
    place_rows = lax.broadcasted_iota(jnp.int32, (256, BLOCK), 0)
    send_rows = lax.broadcasted_iota(jnp.int32, (16 * STRIDE, BLOCK), 0)
    spot = jnp.zeros((256, BLOCK), F32)
    own = [jnp.zeros((16 * STRIDE, BLOCK), F32) for _ in range(2)]
    weight = jnp.zeros((16 * STRIDE, BLOCK), F32)
    for k in range(2):
        slot = jnp.sum(earlier * hit[k], axis=0, keepdims=True).astype(jnp.int32)
        upper = (slot >= HALF).astype(jnp.int32)
        slot = slot - HALF * upper
        name = ids[k : k + 1, :]
        away = jnp.where(upper == tp, 0, 4096)
        spot = spot + (place_rows == name * 16 + slot + away).astype(F32)
        for h in range(2):
            mark = (send_rows == name * STRIDE + h * HALF + slot + away).astype(F32)
            own[h] = own[h] + mark
            weight = weight + mark * weights[k : k + 1, :]
    spots[...] = spot.astype(BF)
    scale = jnp.sum(weight, axis=1, keepdims=True)
    own = [o.astype(BF) for o in own]
    for n in range(8):
        copies[n].wait()
        part = slice(n * 16, (n + 1) * 16)
        hid = hid_rows[part, :].astype(F32)
        inverse = lax.rsqrt(jnp.mean(hid * hid, axis=1, keepdims=True) + EPSILON)
        mixed[part, :] = (hid * inverse * gain[...][None, :]).astype(BF)
    for copy in copies[8:]:
        copy.wait()

    @pl.when(y < 2)
    def _():
        at = (y % 2) * 2 * PIECE
        first = pl.ds(pl.multiple_of(at, PIECE), PIECE)
        second = pl.ds(pl.multiple_of(at + PIECE, PIECE), PIECE)
        rows = nn(own[0], mixed[:, first]) + nn(own[1], mixed[:, second])
        send[...] = rows.reshape(16, STRIDE, PIECE).astype(BF)

    @pl.when(y >= 2)
    def _():
        rows = (nn(own[0], grad_rows[:, :PIECE]) + nn(own[1], grad_rows[:, PIECE:])) * scale
        send[...] = rows.reshape(16, STRIDE, PIECE).astype(BF)


def compact_kernel(came, out):
    rows = came[...].astype(F32).reshape(16 * STRIDE, PIECE).astype(BF)
    to = lax.broadcasted_iota(jnp.int32, (320, 16 * STRIDE), 0)
    at = lax.broadcasted_iota(jnp.int32, (320, 16 * STRIDE), 1)
    block = at // STRIDE
    place = at - block * STRIDE
    half = (place >= HALF).astype(jnp.int32)
    pick = ((to == half * 160 + block * HALF + place - half * HALF) & (place < 2 * HALF)).astype(BF)
    out[...] = nn(pick, rows).astype(BF)


def gate_grads(a, b, back):
    s = jax.nn.sigmoid(a)
    ga = (back * b * s * (1.0 + a * (1.0 - s))).astype(BF)
    gb = (back * a * s).astype(BF)
    return ga, gb


def hidden_grads(x, y, gate, up, down):
    return gate_grads(nt(x, gate), nt(x, up), nt(y, down))


def piece_lanes(index):
    return pl.ds(pl.multiple_of(index * PIECE, PIECE), PIECE)


def dense_kernel(me, mixed, grad_out, gate_in, up_in, down_in, *refs):
    outs, (grad_rows, gate, up, down, sems) = refs[:4], refs[4:]
    copies = []
    for source, target in ((gate_in, gate), (up_in, up), (grad_out, grad_rows), (down_in, down)):
        for start in range(0, D, PIECE):
            part = pl.ds(start, PIECE)
            copies.append(pltpu.make_async_copy(source.at[:, part], target.at[:, part], sems.at[len(copies)]))
            copies[-1].start()
    for copy in copies[:4]:
        copy.wait()
    a = nt(mixed[...], gate[...])
    for copy in copies[4:8]:
        copy.wait()
    b = nt(mixed[...], up[...])
    for copy in copies[8:]:
        copy.wait()
    ga, gb = gate_grads(a, b, nt(grad_rows[...], down[...]))
    y = me[2] // 2
    for d, out in enumerate(outs):
        lanes = piece_lanes((y + d) % 4)
        out[...] = (nn(ga, gate[:, lanes]) + nn(gb, up[:, lanes])).astype(BF)


def load_kernel(*refs):
    count = (len(refs) - 1) // 2
    sems = refs[-1]
    copies = []
    for source, target in zip(refs[:count], refs[count:-1]):
        for n in range(3):
            part = pl.ds(n * 80, 80)
            copies.append(pltpu.make_async_copy(source.at[part], target.at[part], sems.at[len(copies)]))
            copies[-1].start()
    for copy in copies:
        copy.wait()


def expert_kernel(me, own, right, left, far0, far1, gate, up, down, gate2, up2, down2, *refs):
    outs, rows = refs[:4], refs[4]
    y = me[2] // 2
    for h in range(2):
        part = slice(h * 160, (h + 1) * 160)
        rows[:, piece_lanes(y * 2 + h)] = own[part, :]
        rows[:, piece_lanes((y + 3) % 4 * 2 + h)] = right[part, :]
        rows[:, piece_lanes((y + 1) % 4 * 2 + h)] = left[part, :]
    rows[:, piece_lanes((y + 2) % 4 * 2)] = far0[...]
    rows[:, piece_lanes((y + 2) % 4 * 2 + 1)] = far1[...]
    x, g = rows[:, :D], rows[:, D:]
    ga, gb = hidden_grads(x, g, gate[...], up[...], down[...])
    ga2, gb2 = hidden_grads(x, g, gate2[...], up2[...], down2[...])
    for d, out in enumerate(outs):
        lanes = piece_lanes((y + d) % 4)
        total = nn(ga, gate[:, lanes]) + nn(gb, up[:, lanes])
        total = total + (nn(ga2, gate2[:, lanes]) + nn(gb2, up2[:, lanes]))
        out[...] = total.astype(BF)


def sum_kernel(me, first, second, third, fourth, keep, give):
    z = me[2] % 2
    for side, out in ((z, keep), (1 - z, give)):
        lanes = pl.ds(pl.multiple_of(side * (PIECE - CHUNK), 128), CHUNK)
        total = first[:, lanes].astype(F32) + second[:, lanes].astype(F32)
        total = total + third[:, lanes].astype(F32) + fourth[:, lanes].astype(F32)
        out[...] = total.astype(BF)


def expand_kernel(keep, came, out):
    total = (keep[...].astype(F32) + came[...].astype(F32)).astype(BF)
    to = lax.broadcasted_iota(jnp.int32, (256, 160), 0)
    at = lax.broadcasted_iota(jnp.int32, (256, 160), 1)
    block = to // 16
    slot = to - block * 16
    pick = ((at == block * HALF + slot) & (slot < HALF)).astype(BF)
    out[...] = nn(pick, total).astype(BF)


def combine_kernel(me, spots, rows, dense_keep, dense_came, keep, give):
    tp = me[1]
    for half, out in ((tp, keep), (1 - tp, give)):
        lanes = pl.ds(pl.multiple_of(half * 256, 256), 256)
        total = tn(spots[...], rows[:, lanes]) + dense_keep[:, lanes].astype(F32) + dense_came[:, lanes].astype(F32)
        out[...] = total.astype(out.dtype)


def split3(x):
    hi = x.astype(BF).astype(F32)
    mid = (x - hi).astype(BF).astype(F32)
    return hi, mid, x - hi - mid


def norm_kernel(
    me, hidden, grad_out, gain, mine, other, proj_in, stats, heads_out, grad_hidden, message, total, out_proj, sems
):
    copies = []
    for n in range(8):
        part = pl.ds(n * 32, 32)
        copies.append(pltpu.make_async_copy(proj_in.at[part], out_proj.at[part], sems.at[n]))
        copies[-1].start()
    tp = me[1]
    for n in range(8):
        at = (n // 2) * PIECE + (n % 2) * (PIECE - CHUNK)
        total[:, pl.ds(pl.multiple_of(at + tp * 256, 128), 256)] = mine[n]
        total[:, pl.ds(pl.multiple_of(at + (1 - tp) * 256, 128), 256)] = other[n]
    hid = hidden[...].astype(F32)
    inverse = lax.rsqrt(jnp.mean(hid * hid, axis=1, keepdims=True) + EPSILON)
    normed = hid * inverse
    scaled = total[...].astype(F32) * gain[...][None, :]
    mean = jnp.mean(scaled * normed, axis=1, keepdims=True)
    grad = (grad_out[...].astype(F32) + inverse * (scaled - normed * mean)).astype(BF)
    grad_hidden[...] = grad
    for copy in copies:
        copy.wait()
    heads = nt(grad, out_proj[...]).astype(BF)
    rows = []
    for h in range(2):
        heads_t = jnp.transpose(heads[:, head(h)].astype(F32))
        delta = jnp.sum(heads_t * heads_out[h], axis=0, keepdims=True)
        rows.append(list(split3(stats[h : h + 1, :])) + list(split3(delta)))
    extra = jnp.concatenate(
        [jnp.concatenate([rows[0][k], rows[1][k]], axis=1) for k in range(6)] + [jnp.zeros((10, 256), F32)], axis=0
    ).astype(BF)
    for n in range(4):
        message[n, :BLOCK, :] = heads
        message[n, BLOCK:, :] = extra


def stats_kernel(me, own, gathered, stats, heads_out):
    block = me[0]
    key_at = lax.broadcasted_iota(jnp.int32, (2048, BLOCK), 0)
    query_at = lax.broadcasted_iota(jnp.int32, (2048, BLOCK), 1) + block * BLOCK
    allowed = key_at <= query_at
    lines = []
    for h in range(2):
        lanes = slice(h * HEAD_DIM, (h + 1) * HEAD_DIM)
        keys = gathered[:, 256 + h * HEAD_DIM : 256 + (h + 1) * HEAD_DIM]
        values = gathered[:, 512 + h * HEAD_DIM : 512 + (h + 1) * HEAD_DIM]
        scores = jnp.where(allowed, nt(keys, own[:, lanes]) * HEAD_DIM ** (-0.5), NEG_FILL)
        top = jnp.max(scores, axis=0, keepdims=True)
        weights = jnp.where(allowed, jnp.exp(scores - top), 0.0)
        lines.append(top + jnp.log(jnp.sum(weights, axis=0, keepdims=True)))
        half = weights.astype(BF)
        heads_out[h] = tn(values, half) / jnp.sum(half.astype(F32), axis=0, keepdims=True)
    stats[...] = jnp.concatenate(lines + [jnp.zeros((6, BLOCK), F32)], axis=0)


def pair(keys, values, queries, upstream, lines, allowed):
    log_norm = lines[0:1] + lines[1:2] + lines[2:3]
    delta = lines[3:4] + lines[4:5] + lines[5:6]
    probs = jnp.where(allowed, jnp.exp(nt(keys, queries) * SCALE - log_norm), 0.0)
    grad_scores = probs * (nt(values, upstream) - delta)
    return probs.astype(BF), grad_scores.astype(BF)


def head(h, start=0):
    return slice(start + h * HEAD_DIM, start + (h + 1) * HEAD_DIM)


def queries_kernel(me, own_q, gathered, grads, grad_q, total):
    block = me[0]
    message = grads.at[block // 4]
    lines = message[BLOCK:, :].astype(F32)
    query_at = lax.broadcasted_iota(jnp.int32, (512, BLOCK), 1) + block * BLOCK
    total[...] = jnp.zeros_like(total)
    for i in range(4):

        @pl.when(4 * i <= block)
        def _(i=i):
            rows = slice(i * 512, (i + 1) * 512)
            allowed = lax.broadcasted_iota(jnp.int32, (512, BLOCK), 0) + i * 512 <= query_at
            for h in range(2):
                keys = gathered[rows, head(h, 256)]
                values = gathered[rows, head(h, 512)]
                _, half = pair(keys, values, own_q[:, head(h)], message[:BLOCK, head(h)], lines[:, head(h)], allowed)
                total[:, head(h)] += tn(half, keys)

    grad_q[...] = (total[...] * SCALE).astype(BF)


def keys_kernel(shifts, first, last, me, gathered, *refs):
    count = len(shifts)
    grads, refs = refs[:count], refs[count:]
    if first:
        out_k, out_v, sum_k, sum_v = refs
        sum_k[...] = jnp.zeros_like(sum_k)
        sum_v[...] = jnp.zeros_like(sum_v)
    else:
        in_k, in_v, out_k, out_v, sum_k, sum_v = refs
        sum_k[...] = in_k[...]
        sum_v[...] = in_v[...]
    block = me[0]
    own_rows = pl.ds(pl.multiple_of(block * BLOCK, BLOCK), BLOCK)
    lane = lax.broadcasted_iota(jnp.int32, (BLOCK, 4 * BLOCK), 1)
    key_at = lax.broadcasted_iota(jnp.int32, (BLOCK, 4 * BLOCK), 0) + block * BLOCK
    for shift, source in zip(shifts, grads):
        column = (block + shift) % 4
        allowed = key_at <= (lane // BLOCK * 4 + column) * BLOCK + lane % BLOCK
        blocks = [n * 4 + column for n in range(4)]
        queries = jnp.concatenate(
            [gathered[pl.ds(pl.multiple_of(i * BLOCK, BLOCK), BLOCK), :256] for i in blocks], axis=0
        )
        upstream = jnp.concatenate([source[n, :BLOCK, :] for n in range(4)], axis=0)
        lines = [source[n, BLOCK:, :].astype(F32) for n in range(4)]
        for h in range(2):
            line = jnp.concatenate([part[:, head(h)] for part in lines], axis=1)
            keys = gathered[own_rows, head(h, 256)]
            values = gathered[own_rows, head(h, 512)]
            probs, half = pair(keys, values, queries[:, head(h)], upstream[:, head(h)], line, allowed)
            sum_k[:, head(h)] += nn(half, queries[:, head(h)])
            sum_v[:, head(h)] += nn(probs, upstream[:, head(h)])

    if last:
        out_k[...] = (sum_k[...] * SCALE).astype(BF)
        out_v[...] = sum_v[...].astype(BF)
    else:
        out_k[...] = sum_k[...]
        out_v[...] = sum_v[...]


def shape(*dims, kind=BF):
    return jax.ShapeDtypeStruct(dims, kind)


def body(
    hidden,
    grad_out,
    gain,
    dense_gate,
    dense_up,
    dense_down,
    expert_gate,
    expert_up,
    expert_down,
    out_proj,
    queries,
    keys,
    values,
    route_ids,
    route_weights,
):
    me = jnp.stack([lax.axis_index("ctx"), lax.axis_index("tp"), lax.axis_index("ep")]).astype(jnp.int32)
    experts = [expert_gate[0], expert_up[0], expert_down[0]]

    mixed, send, spots, heads = call(
        prepare_kernel,
        (shape(BLOCK, D), shape(16, STRIDE, PIECE), shape(256, BLOCK), shape(BLOCK, 768)),
        [SMEM, HBM, HBM, VMEM, VMEM, VMEM, HBM, HBM, HBM],
        scratch=[pltpu.VMEM((BLOCK, D), BF), pltpu.VMEM((BLOCK, 2 * PIECE), BF), pltpu.SemaphoreType.DMA((15,))],
        flops=10**8,
        bytes_accessed=4 * 10**6,
        mib=16,
        name="prepare",
    )(me, in_hbm(hidden), in_hbm(grad_out), gain, route_ids.T, route_weights.T, *[in_hbm(w) for w in (queries, keys, values)])
    gathered = lax.all_gather(heads, "ctx", axis=0, tiled=True)
    came = lax.all_to_all(send, "ctx", split_axis=0, concat_axis=0, tiled=True)

    dense = call(
        dense_kernel,
        (shape(BLOCK, PIECE),) * 4,
        [SMEM, VMEM] + [HBM] * 4,
        scratch=[pltpu.VMEM((BLOCK, D), BF)] + [pltpu.VMEM((152, D), BF)] * 3 + [pltpu.SemaphoreType.DMA((16,))],
        flops=10 * 128 * 152 * D,
        bytes_accessed=6 * 10**6,
        mib=16,
        name="dense",
    )(me, mixed, *[in_hbm(w) for w in (grad_out, dense_gate, dense_up, dense_down)])
    peers = [to_tp(w) for w in experts]
    dense_keep, dense_give = sum_over_y(me, dense, "dense_sum")

    came, dense_keep, dense_give = lax.optimization_barrier((came, dense_keep, dense_give))
    own = call(compact_kernel, shape(320, PIECE), [VMEM], name="compact")(came)
    right, left = to_ep(own, 1, 0), to_ep(own, -1, 0)
    far = [to_ep(right[:160], 1, 0), to_ep(left[160:], -1, 0)]
    *weights, _ = lax.optimization_barrier((*experts, *peers, own))
    weights = call(
        load_kernel,
        (shape(240, D),) * 6,
        [HBM] * 6,
        scratch=[pltpu.SemaphoreType.DMA((18,))],
        bytes_accessed=10**7,
        name="load",
    )(*[in_hbm(w) for w in weights])
    parts = call(
        expert_kernel,
        (shape(160, PIECE),) * 4,
        [SMEM] + [VMEM] * 11,
        scratch=[pltpu.VMEM((160, 2 * D), BF)],
        mib=16,
        flops=10 * 320 * 240 * D,
        bytes_accessed=18 * 10**6,
        name="expert",
    )(me, own, right, left, *far, *weights)
    keep, give = sum_over_y(me, parts, "sum")
    back = call(expand_kernel, shape(256, CHUNK), [VMEM] * 2, name="expand")(keep, to_ep(give, 0, 1))
    back = lax.all_to_all(back.reshape(16, 16, CHUNK), "ctx", split_axis=0, concat_axis=0, tiled=True)

    stats, heads_out = call(
        stats_kernel,
        (shape(8, BLOCK, kind=F32), shape(2, HEAD_DIM, BLOCK, kind=F32)),
        [SMEM] + [VMEM] * 2,
        flops=4 * 2 * 2048 * 128 * 128,
        bytes_accessed=4 * 10**6,
        mib=16,
        name="stats",
    )(me, queries, gathered)

    back, stats, heads_out, dense_came = lax.optimization_barrier((back, stats, heads_out, to_ep(dense_give, 0, 1)))
    keep, give = call(
        combine_kernel,
        (shape(BLOCK, 256, kind=F32), shape(BLOCK, 256)),
        [SMEM] + [VMEM] * 4,
        name="combine",
    )(me, spots, back.reshape(256, CHUNK), dense_keep, dense_came)
    total = (keep + to_tp(give).astype(F32)).astype(BF)
    total = jnp.broadcast_to(total[None], (8, BLOCK, 256))
    total = lax.all_to_all(total, "ep", split_axis=0, concat_axis=0, tiled=True)
    grad_hidden, message = call(
        norm_kernel,
        (shape(BLOCK, D), shape(4, GRAY, 256)),
        [SMEM, VMEM, VMEM, VMEM, VMEM, VMEM, HBM, VMEM, VMEM],
        scratch=[pltpu.VMEM((BLOCK, D), BF), pltpu.VMEM((256, D), BF), pltpu.SemaphoreType.DMA((8,))],
        flops=4 * 128 * 256 * D,
        bytes_accessed=6 * 10**6,
        mib=16,
        name="norm",
    )(me, hidden, grad_out, gain, total, to_tp(total), in_hbm(out_proj), stats, heads_out)
    column = lax.all_to_all(message, "ctx", split_axis=0, concat_axis=0, tiled=True, axis_index_groups=COLUMNS)
    grad_q = call(
        queries_kernel,
        shape(BLOCK, 256),
        [SMEM] + [VMEM] * 3,
        scratch=[pltpu.VMEM((BLOCK, 256), F32)],
        flops=8 * 2 * 3 * 2 * 128**3,
        bytes_accessed=4 * 10**6,
        mib=16,
        name="queries",
    )(me, queries, gathered, column)

    def keys_part(shifts, columns, sums, first, last):
        return call(
            functools.partial(keys_kernel, shifts, first, last),
            (shape(BLOCK, 256, kind=BF if last else F32),) * 2,
            [SMEM] + [VMEM] * (1 + len(columns) + len(sums)),
            scratch=[pltpu.VMEM((BLOCK, 256), F32)] * 2,
            flops=4 * len(shifts) * 2 * 4 * 2 * 128**3,
            bytes_accessed=4 * 10**6,
            mib=16,
        name="keys",
        )(me, gathered, *columns, *sums)

    opposite = to_ctx(column, 2)
    beside = [to_ctx(column, -1), to_ctx(column, 1)]
    sums = keys_part((0,), [column], [], True, False)
    sums = keys_part((2,), [opposite], sums, False, False)
    grad_k, grad_v = keys_part((1, 3), beside, sums, False, True)
    return grad_hidden, grad_q, grad_k, grad_v


def solution(mesh):
    return jax.shard_map(
        body,
        mesh=mesh,
        in_specs=(
            P("ctx", None),
            P("ctx", None),
            P(),
            P(("tp", "ep"), None),
            P(("tp", "ep"), None),
            P(("tp", "ep"), None),
            P("ctx", ("tp", "ep"), None),
            P("ctx", ("tp", "ep"), None),
            P("ctx", ("tp", "ep"), None),
            P(("tp", "ep"), None),
            P("ctx", ("tp", "ep")),
            P("ctx", ("tp", "ep")),
            P("ctx", ("tp", "ep")),
            P("ctx", None),
            P("ctx", None),
        ),
        out_specs=(
            P("ctx", None),
            P("ctx", ("tp", "ep")),
            P("ctx", ("tp", "ep")),
            P("ctx", ("tp", "ep")),
        ),
        check_vma=False,
    )
```
